512 devices in a mesh: expert: 64 (over x, z, core), dp: 8 (over y).
Axes of the slice: x: 4, y: 8, z: 8, core: 2. Of those that a mesh axis runs over, the one named last changes fastest.
Arguments:
- tokens: bfloat16 [1024, 7168], P('expert'), may hold values from -6 to 6
- teacher_out: bfloat16 [1024, 8, 7168], P('expert', None, 'dp'), may hold values from -4 to 4
- route_weight: bfloat16 [1024, 8], P('expert'), may hold values from 0.049804688 to 0.5
- routes: int32 [1024, 8], P('expert'), may hold values from 0 to 63, all different within a row; in each aligned block of 16 rows (0 to 15, 16 to 31, ...) at most 4 rows name the same one
- twin_map: int32 [64], replicated, may hold values from 0 to 31, as said below
- student_gate: bfloat16 [64, 384, 7168], P('expert', 'dp'), may hold values from -0.0625 to 0.0625
- student_up: bfloat16 [64, 384, 7168], P('expert', 'dp'), may hold values from -0.0625 to 0.0625
- student_down: bfloat16 [64, 384, 7168], P('expert', None, 'dp'), may hold values from -0.21875 to 0.21875
Outputs:
- grad_gate: bfloat16 [64, 384, 7168], P('expert', 'dp')
- grad_up: bfloat16 [64, 384, 7168], P('expert', 'dp')
- grad_down: bfloat16 [64, 384, 7168], P('expert', None, 'dp')
The draws below stay inside these ranges and needn't reach their ends.
Inputs may be any that keep to these rules, and one draw needn't show every extreme that they name: `routes`: in the 16 tokens held by one device of the expert axis (one routing block) no teacher expert is named more than 4 times, and each token names 8 different teacher experts. `twin_map`: each student number is named by exactly two teacher experts.
All inputs are finite; a program needn't handle non-finite values.
Results may differ from the reference program's by a relative error of at most 0.024.
Values may be sent and summed in bfloat16 or wider, within the bound.
A program may use at most 128 MiB of HBM per device.

```python
import math
import jax
import jax.numpy as jnp
import numpy as np
from jax import lax

D = 7168
FF_S = 768
TOPK = 8
TOK_E = 16
NT = 64
NS = 32
CAP = 4
SLOTS = 512
TOKENS = 1024


def draw_twin_map(key, part):
    key = jax.random.fold_in(key, 7)
    shuffled = jax.random.permutation(key, NT)
    return (shuffled // 2).astype(jnp.int32)


def steps_of(stream_key, shape, split, least, high):
    def one(dim, blocks):
        heights = jax.random.uniform(jax.random.fold_in(jax.random.fold_in(stream_key, 6), dim), (blocks,), jnp.float32, least / len(split), high / len(split))
        return jnp.repeat(jnp.exp(heights), shape[dim] // blocks).reshape((-1,) + (1,) * (len(shape) - dim - 1))

    loudness = one(*split[0])
    for cut in split[1:]:
        loudness = loudness * one(*cut)
    return loudness


def routed_block(rng, own, number, rows, number_of, top, limit, lean):
    ranking = jax.random.permutation(rng, number_of)
    packed, common = load_shares(number_of, rows * top, limit, lean, True), load_shares(number_of, rows * top, limit, lean, False)
    places = jnp.arange(number_of)

    def named(lengths, rotation):
        used = int((lengths > 0).sum())
        fixed = max(1, used // 4)
        shifted = fixed + (places - fixed + rotation * (used - fixed)) % max(1, number_of - fixed)
        return jnp.zeros((number_of,), jnp.int32).at[ranking[jnp.where(places < fixed, places, shifted)]].set(jnp.asarray(lengths, jnp.int32))

    lengths = jnp.where(number % 4 == 0, named(packed, number // 4), named(common, number - number // 4 - 1))
    mixed = jax.random.permutation(jax.random.fold_in(own, 3), number_of)
    donor, taker = mixed[0:number_of // 2 * 2:2], mixed[1:number_of // 2 * 2:2]
    margin = jnp.minimum(lengths[donor] - 1, limit - lengths[taker]) // 2
    margin = jnp.where((donor == ranking[0]) | (taker == ranking[0]) | (lengths[taker] == 0), 0, jnp.maximum(margin, 0))
    shifted = jax.random.randint(jax.random.fold_in(own, 4), (number_of // 2,), 0, 1 << 20) % (margin + 1)
    lengths = lengths.at[donor].add(-shifted).at[taker].add(shifted)
    members = jnp.searchsorted(jnp.cumsum(lengths), jnp.arange(rows * top), side="right").astype(jnp.int32)
    listing = members.reshape(top, rows).T
    listing = listing[jax.random.permutation(jax.random.fold_in(own, 1), rows)]
    rotation = jax.random.randint(jax.random.fold_in(own, 2), (rows, 1), 0, top)
    return jnp.take_along_axis(listing, (jnp.arange(top)[None, :] + rotation) % top, axis=1)


def load_shares(amount, total, reach, skew, full):
    portions = [(1 << 20) // math.isqrt(standing ** skew) + 1 for standing in range(1, amount + 1)]
    largest = reach if full else min(reach, max(-(-total // amount), total * portions[0] // sum(portions)))
    least = 1 if total - largest >= amount - 1 else 0
    counts, surplus = [largest] + [least] * (amount - 1), total - largest - least * (amount - 1)
    while surplus > 0:
        movable = [i for i in range(1, amount) if counts[i] < largest] or [i for i in range(1, amount) if counts[i] < reach]
        pool, budget = sum([portions[i] for i in movable]), surplus
        for i in movable:
            addition = min(reach - counts[i], max(1, budget * portions[i] // pool), surplus)
            counts[i] = counts[i] + addition
            surplus = surplus - addition
    return np.array(counts)


def gaussian(own_key, shape, deviation, bound, shards=(), held_as=jnp.bfloat16):
    entries = deviation * jax.random.normal(own_key, shape, jnp.float32)
    if shards:
        entries = entries * steps_of(own_key, shape, shards, -0.22, 0.18)
    return jnp.clip(entries, -bound, bound).astype(held_as)


def setup_inputs(seed: int = 0) -> dict:
    key_of = jax.random.split(jax.random.key(seed), 9)
    tokens = gaussian(key_of[0], (TOKENS, D), 1.0, 6.0, ((0, 64),))
    teacher_out = gaussian(key_of[1], (TOKENS, TOPK, D), 0.5, 4.0, ((0, 64), (2, 8)))
    route_weight = jnp.clip(jnp.exp(math.log(0.5) - 2.306499 * jax.random.uniform(key_of[2], (TOKENS, TOPK), jnp.float32) ** steps_of(key_of[2], (TOKENS, TOPK), ((0, 64),), -0.2, 0.2)), 0.049804688, 0.5).astype(jnp.bfloat16)
    routes_keys = jax.random.split(jax.random.fold_in(key_of[3], 1), TOKENS // TOK_E)
    routes_turns = jax.random.permutation(jax.random.fold_in(key_of[3], 3), TOKENS // TOK_E)
    routes = jax.vmap(lambda own, number: routed_block(jax.random.fold_in(key_of[3], 2), own, number, TOK_E, NT, TOPK, CAP, 2))(routes_keys, routes_turns).reshape((TOKENS, TOPK))
    twin_map = draw_twin_map(jax.random.fold_in(key_of[8], 71), 0)
    student_gate = gaussian(key_of[5], (NT, FF_S // 2, D), D ** -0.5, 0.0625, ((0, 64), (1, 8)))
    student_up = gaussian(key_of[6], (NT, FF_S // 2, D), D ** -0.5, 0.0625, ((0, 64), (1, 8)))
    student_down = gaussian(key_of[7], (NT, FF_S // 2, D), FF_S ** -0.5, 0.21875, ((0, 64), (2, 8)))
    return dict(tokens=tokens, teacher_out=teacher_out, route_weight=route_weight, routes=routes, twin_map=twin_map, student_gate=student_gate, student_up=student_up, student_down=student_down)


def twin_positions(twin_map):
    teacher_count = twin_map.shape[0]
    same_student = twin_map[:, None] == twin_map[None, :]
    earlier = jnp.arange(teacher_count, dtype=jnp.int32)[None, :] < jnp.arange(teacher_count, dtype=jnp.int32)[:, None]
    return jnp.sum(same_student & earlier, axis=1).astype(jnp.int32)


def block_ranks(teach_ids):
    pair_count = teach_ids.shape[-1]
    same_teacher = teach_ids[:, :, None] == teach_ids[:, None, :]
    earlier = jnp.arange(pair_count, dtype=jnp.int32)[None, :] < jnp.arange(pair_count, dtype=jnp.int32)[:, None]
    return jnp.sum(same_teacher & earlier[None], axis=2).astype(jnp.int32)


def swiglu_grads(rows_x, rows_target, rows_weight, w_gate, w_up, w_down):
    gate_pre = jnp.dot(rows_x, w_gate.T, preferred_element_type=jnp.float32)
    up_pre = jnp.dot(rows_x, w_up.T, preferred_element_type=jnp.float32)
    sigmoid_gate = jax.nn.sigmoid(gate_pre)
    silu_gate = gate_pre * sigmoid_gate
    hidden = (silu_gate * up_pre).astype(jnp.bfloat16)
    student_out = jnp.dot(hidden, w_down, preferred_element_type=jnp.float32)
    error_rows = (rows_weight.astype(jnp.float32)[:, None] * (student_out - rows_target.astype(jnp.float32))).astype(jnp.bfloat16)
    grad_down = jnp.dot(hidden.T, error_rows, preferred_element_type=jnp.float32).astype(jnp.bfloat16)
    back_hidden = jnp.dot(error_rows, w_down.T, preferred_element_type=jnp.float32)
    silu_slope = sigmoid_gate * (1.0 + gate_pre * (1.0 - sigmoid_gate))
    back_gate = (back_hidden * up_pre * silu_slope).astype(jnp.bfloat16)
    back_up = (back_hidden * silu_gate).astype(jnp.bfloat16)
    grad_gate = jnp.dot(back_gate.T, rows_x, preferred_element_type=jnp.float32).astype(jnp.bfloat16)
    grad_up = jnp.dot(back_up.T, rows_x, preferred_element_type=jnp.float32).astype(jnp.bfloat16)
    return grad_gate, grad_up, grad_down


def one_student(inputs):
    return swiglu_grads(*inputs)


def reference(tokens, teacher_out, route_weight, routes, twin_map, student_gate, student_up, student_down):
    pair_count = TOK_E * TOPK
    teach_ids = routes.reshape(NT, pair_count).astype(jnp.int32)
    student_ids = twin_map[teach_ids].astype(jnp.int32)
    twin_ids = twin_positions(twin_map)[teach_ids].astype(jnp.int32)
    rank_ids = block_ranks(teach_ids)
    blocks = jnp.arange(NT, dtype=jnp.int32)[:, None]
    slot_ids = (student_ids * SLOTS + blocks * (2 * CAP) + twin_ids * CAP + rank_ids).reshape(-1).astype(jnp.int32)
    pair_rows = jnp.repeat(tokens, TOPK, axis=0)
    rows_x = jnp.zeros((NS * SLOTS, D), jnp.bfloat16).at[slot_ids].set(pair_rows)
    rows_target = jnp.zeros((NS * SLOTS, D), jnp.bfloat16).at[slot_ids].set(teacher_out.reshape(TOKENS * TOPK, D))
    rows_weight = jnp.zeros((NS * SLOTS,), jnp.bfloat16).at[slot_ids].set(route_weight.reshape(TOKENS * TOPK))
    gradients = lax.map(one_student, (rows_x.reshape(NS, SLOTS, D), rows_target.reshape(NS, SLOTS, D), rows_weight.reshape(NS, SLOTS), student_gate.reshape(NS, FF_S, D), student_up.reshape(NS, FF_S, D), student_down.reshape(NS, FF_S, D)))
    return (gradients[0].reshape(NT, FF_S // 2, D), gradients[1].reshape(NT, FF_S // 2, D), gradients[2].reshape(NT, FF_S // 2, D))
```

```python
import functools
import jax
import jax.numpy as jnp
from jax import lax
from jax.experimental import pallas as pl
from jax.experimental.pallas import tpu as pltpu
from jax.sharding import PartitionSpec as P

BF = jnp.bfloat16
F32 = jnp.float32
XS = 4
NT_DIMS = (((1,), (1,)), ((), ()))
TN_DIMS = (((0,), (0,)), ((), ()))


def hot(cond):
    return jnp.where(cond, 1.0, 0.0).astype(BF)


def iota(shape, dim):
    return lax.broadcasted_iota(jnp.int32, shape, dim)


def target_width(feature):
    return -(-(feature + 128) // 256) * 128


def pack_kernel(tokens, teacher, weight, routes, twin_col, twin_row, pay_rows, pay_target):
    block, topk = routes.shape
    pairs = block * topk
    teachers = twin_col.shape[0]
    cap = 2 * pairs // teachers
    group = 2 * cap
    feature = teacher.shape[2]
    width = target_width(feature)
    rows = pay_rows.shape[0] * pay_rows.shape[1]
    cls = lax.rem(lax.axis_index("dp"), 4)

    token_of = hot(iota((pairs, block), 0) // topk == iota((pairs, block), 1))
    token_of_t = hot(iota((block, pairs), 1) // topk == iota((block, pairs), 0))
    place_col = iota((pairs, topk), 0) % topk == iota((pairs, topk), 1)
    place_row = iota((topk, pairs), 1) % topk == iota((topk, pairs), 0)
    named = routes[...].astype(F32).astype(BF)
    teach_col = jnp.sum(
        jnp.where(place_col, jnp.dot(token_of, named, preferred_element_type=F32), 0.0),
        axis=1, keepdims=True)
    teach_row = jnp.sum(
        jnp.where(place_row, lax.dot_general(named, token_of_t, TN_DIMS, preferred_element_type=F32), 0.0),
        axis=0, keepdims=True)
    weight_col = jnp.sum(
        jnp.where(place_col, jnp.dot(token_of, weight[...], preferred_element_type=F32), 0.0),
        axis=1, keepdims=True)
    earlier = iota((pairs, pairs), 0) < iota((pairs, pairs), 1)
    rank_row = jnp.sum(
        jnp.where((teach_col == teach_row) & earlier, 1.0, 0.0), axis=0, keepdims=True)
    twins = twin_col[...] == twin_row[...]
    before = iota((teachers, teachers), 1) < iota((teachers, teachers), 0)
    twin_of = jnp.sum(jnp.where(twins & before, 1.0, 0.0), axis=1, keepdims=True)
    first_slot = twin_col[...].astype(F32) * float(group) + twin_of * float(cap)
    teacher_hot = iota((teachers, pairs), 0).astype(F32) == teach_row
    slot_row = rank_row + jnp.sum(jnp.where(teacher_hot, first_slot, 0.0), axis=0, keepdims=True)

    row_ids = iota((rows, pairs), 0)
    slot_of = (row_ids // (2 * group)) * group + row_ids % group
    half_of = (row_ids // group) % 2
    filled = slot_of.astype(F32) == slot_row
    put_low = hot(filled & (half_of == 0))
    put_high = hot(filled & (half_of == 1))

    spread = hot(iota((pairs, 2 * block), 0) // topk == iota((pairs, 2 * block), 1) % block)
    pick = jnp.dot(hot(filled), spread, preferred_element_type=F32)
    pick_half = iota((rows, 2 * block), 1) // block == (iota((rows, 2 * block), 0) // group) % 2
    pick = jnp.where(pick_half, pick, 0.0).astype(BF)
    low = tokens[:, pl.ds(pl.multiple_of(cls * feature, 128), feature)]
    high = tokens[:, pl.ds(pl.multiple_of((cls + 4) * feature, 128), feature)]
    both = jnp.concatenate([low, high], axis=0)
    sent = jnp.dot(pick, both, preferred_element_type=F32).astype(BF)
    pay_rows[...] = sent.reshape(pay_rows.shape)

    target = teacher[...].astype(F32).reshape(pairs, feature).astype(BF)
    spread_weight = jnp.broadcast_to(weight_col, (pairs, 128)).astype(BF)
    tail = jnp.concatenate([target[:, width:], spread_weight], axis=1)
    sent = jnp.dot(put_low, target[:, :width], preferred_element_type=F32) + jnp.dot(
        put_high, tail, preferred_element_type=F32)
    pay_target[...] = sent.astype(BF).reshape(pay_target.shape)


def main_kernel(
    pay_rows, pay_target, gate, up, down,
    grad_gate, grad_up, grad_down,
    rows, target, weights, weights_down, pre, slots_pre, hidden, err, back_out, back_in,
    down_own, down_out, down_in, expand, own, gate_out, gate_in,
    w_recv, w_local, w_send, rows_recv, rows_send, target_recv, target_send,
    left_recv, right_recv, fwd_left_recv, fwd_right_recv, ring_send,
    hid_send, hid_recv, back_send, back_recv, down_send, down_recv, gate_send, gate_recv,
):
    chips = pay_rows.shape[0]
    line = chips // XS
    height = pay_rows.shape[1]
    group = height // 2
    feature = pay_rows.shape[2]
    width = pay_target.shape[2]
    tail = feature - width
    units = gate.shape[0]
    count_y = down.shape[0]
    slots = chips * group
    me = lax.axis_index("expert")
    y = lax.axis_index("dp")
    core = lax.rem(me, 2)
    other = 1 - core
    chip = me // 2
    x = chip // line
    z = lax.rem(chip, line)
    sibling = (chip * 2 + other, y)
    right_y = lax.rem(y + 1, count_y)
    left_y = lax.rem(y + count_y - 1, count_y)
    right = (me, right_y)
    left = (me, left_y)

    def peer(step):
        dx = step // line
        to = lax.rem(x + XS - dx, XS) * line + lax.rem(z + step, line)
        return dx, to

    def remote(src, dst, send_sem, recv_sem, device):
        return pltpu.make_async_remote_copy(
            src_ref=src, dst_ref=dst, send_sem=send_sem, recv_sem=recv_sem,
            device_id=device, device_id_type=pl.DeviceIdType.MESH)

    def await_bytes(ref, sem):
        pltpu.make_async_copy(ref, ref, sem).wait()

    barrier = pltpu.get_barrier_semaphore()
    pl.semaphore_signal(barrier, inc=1, device_id=sibling, device_id_type=pl.DeviceIdType.MESH)

    def greet_chip(step, carry):
        _, to = peer(step)
        pl.semaphore_signal(
            barrier, inc=1, device_id=(to * 2 + core, y), device_id_type=pl.DeviceIdType.MESH)
        return carry

    def greet_y(step, carry):
        pl.semaphore_signal(
            barrier, inc=1, device_id=(me, lax.rem(y + step, count_y)),
            device_id_type=pl.DeviceIdType.MESH)
        return carry

    lax.fori_loop(1, chips, greet_chip, 0)
    lax.fori_loop(1, count_y, greet_y, 0)

    own_copies = [
        pltpu.make_async_copy(gate, weights.at[core, 0], w_local.at[0]),
        pltpu.make_async_copy(up, weights.at[core, 1], w_local.at[1]),
        pltpu.make_async_copy(down, weights_down.at[:, core], w_local.at[2]),
        pltpu.make_async_copy(pay_rows.at[chip], rows.at[0, chip], rows_recv.at[0]),
        pltpu.make_async_copy(pay_target.at[chip], target.at[chip], target_recv),
    ]
    for copy in own_copies:
        copy.start()
    pl.semaphore_wait(barrier, chips - 1 + count_y - 1 + 1)

    def send_rows(step, carry):
        dx, to = peer(step)
        remote(pay_rows.at[to], rows.at[0, chip], rows_send, rows_recv.at[dx], (to * 2 + core, y)).start()
        return carry

    def send_target(step, carry):
        _, to = peer(step)
        remote(pay_target.at[to], target.at[chip], target_send, target_recv, (to * 2 + core, y)).start()
        return carry

    lax.fori_loop(1, chips, send_rows, 0)
    weight_copies = [
        remote(gate, weights.at[core, 0], w_send.at[0], w_recv.at[0], sibling),
        remote(up, weights.at[core, 1], w_send.at[1], w_recv.at[1], sibling),
        remote(down, weights_down.at[:, core], w_send.at[2], w_recv.at[2], sibling),
    ]
    for copy in weight_copies:
        copy.start()
    lax.fori_loop(1, chips, send_target, 0)

    def chunk_at(step):
        return lax.rem(x + step, XS) * line

    def send_own(step):
        at = pl.ds(chunk_at(step), line)
        await_bytes(rows.at[0, at], rows_recv.at[step])
        remote(rows.at[0, at], rows.at[3, at], ring_send.at[0], left_recv.at[step], right).start()
        remote(rows.at[0, at], rows.at[1, at], ring_send.at[1], right_recv.at[step], left).start()

    def forward(step):
        at = pl.ds(chunk_at(step), line)
        first = pl.ds(chunk_at(step), line // 2)
        last = pl.ds(chunk_at(step) + line // 2, line // 2)
        await_bytes(rows.at[3, at], left_recv.at[step])
        remote(rows.at[3, first], rows.at[2, first], ring_send.at[2], fwd_left_recv.at[step], right).start()
        await_bytes(rows.at[1, at], right_recv.at[step])
        remote(rows.at[1, last], rows.at[2, last], ring_send.at[3], fwd_right_recv.at[step], left).start()

    def slice_of(cls):
        return pl.ds(pl.multiple_of(cls * feature, 128), feature)

    def project(step):
        at = chunk_at(step)
        await_bytes(rows.at[2, pl.ds(at, line // 2)], fwd_left_recv.at[step])
        await_bytes(rows.at[2, pl.ds(at + line // 2, line // 2)], fwd_right_recv.at[step])
        pre[...] = jnp.zeros_like(pre)

        def add(rel, carry):
            cls = lax.rem(y + rel, 4)
            part = rows[rel, pl.ds(at, line)].reshape(line * height, feature)
            for half in range(2):
                w = weights[:, :, :, slice_of(cls + 4 * half)].reshape(4 * units, feature)
                pre[half] += lax.dot_general(part, w, NT_DIMS, preferred_element_type=F32)
            return carry

        lax.fori_loop(0, 4, add, 0)
        low = pre[0].reshape(line, height, 4 * units)[:, :group]
        high = pre[1].reshape(line, height, 4 * units)[:, group:]
        first = pl.multiple_of(at * group, group)
        slots_pre[pl.ds(first, line * group), : 4 * units] = (low + high).reshape(line * group, 4 * units)

    slots_pre[...] = jnp.zeros_like(slots_pre)
    send_own(0)
    for copy in own_copies[:3]:
        copy.wait()
    for copy in weight_copies:
        copy.wait()
    for step in range(XS):
        if step + 1 < XS:
            send_own(step + 1)
        forward(step)
        if step > 0:
            project(step - 1)
    project(XS - 1)

    gates = slots_pre[...].T[: 4 * units].reshape(2, 2, units, slots)
    gate_pre = gates[:, 0].reshape(2 * units, slots)
    up_pre = gates[:, 1].reshape(2 * units, slots)
    sig = 1.0 / (1.0 + jnp.exp(-gate_pre))
    silu = gate_pre * sig
    hidden[y] = (silu * up_pre).astype(BF)

    def send_hidden(step, carry):
        to = lax.rem(y + step, count_y)
        remote(hidden.at[y], hidden.at[y], hid_send, hid_recv, (me, to)).start()
        return carry

    lax.fori_loop(1, count_y, send_hidden, 0)
    await_bytes(target, target_recv)
    await_bytes(hidden.at[pl.ds(0, count_y - 1)], hid_recv)

    all_hidden = hidden[...].reshape(count_y * 2 * units, slots)
    all_down = weights_down[...].reshape(count_y * 2 * units, feature)
    out = lax.dot_general(all_hidden, all_down, TN_DIMS, preferred_element_type=F32)
    arrived = target[...].astype(F32)
    goal_low = arrived[:, :group].reshape(slots, width)
    goal_high = arrived[:, group:].reshape(slots, width)
    slot_weight = goal_high[:, tail : tail + 1]
    err[:, :width] = (slot_weight * (out[:, :width] - goal_low)).astype(BF)
    err[:, width:] = (slot_weight * (out[:, width:] - goal_high[:, :tail])).astype(BF)

    def send_back(step, carry):
        to = lax.rem(y + step, count_y)
        w = weights_down[to].reshape(2 * units, feature)
        back_out[to] = lax.dot_general(w, err[...], NT_DIMS, preferred_element_type=F32).astype(BF)

        @pl.when(step < count_y)
        def _():
            remote(back_out.at[to], back_in.at[y], back_send, back_recv, (me, to)).start()
        return carry

    lax.fori_loop(1, count_y + 1, send_back, 0)

    def down_part(part, carry):
        term = jnp.dot(hidden[part], err[...], preferred_element_type=F32)
        down_own[part] = term.reshape(2, units, feature)
        down_out[part] = down_own[part, other].astype(BF)
        return carry

    lax.fori_loop(0, count_y, down_part, 0)
    down_copy = remote(down_out, down_in, down_send, down_recv, sibling)
    down_copy.start()

    await_bytes(back_in.at[pl.ds(0, count_y - 1)], back_recv)
    back_hidden = back_out[y].astype(F32)

    def add_back(step, total):
        return total + back_in[lax.rem(y + step, count_y)].astype(F32)

    back_hidden = lax.fori_loop(1, count_y, add_back, back_hidden)
    slope = sig * (1.0 + gate_pre * (1.0 - sig))
    back_gate = (back_hidden * up_pre * slope).astype(BF).reshape(2, 1, units, slots)
    back_up = (back_hidden * silu).astype(BF).reshape(2, 1, units, slots)
    backs = jnp.concatenate([back_gate, back_up], axis=1).reshape(4 * units, slots)
    wide = (slots, chips * height)
    for half in range(2):
        slot_id, lane = iota(wide, 0), iota(wide, 1)
        match = (lane // height == slot_id // group) & (lane % height == slot_id % group + group * half)
        expand[half] = jnp.dot(backs, hot(match), preferred_element_type=F32).astype(BF)

    def class_part(rel, carry):
        cls = lax.rem(y + rel, 4)
        lhs = expand[...].reshape(8 * units, chips * height)
        part = rows[rel].reshape(chips * height, feature)
        own[rel] = jnp.dot(lhs, part, preferred_element_type=F32).reshape(2, 2, 2 * units, feature)
        gate_out[cls] = own[rel, :, other].astype(BF)
        remote(gate_out.at[cls], gate_in.at[cls], gate_send, gate_recv.at[rel], sibling).start()
        return carry

    lax.fori_loop(0, 4, class_part, 0)

    down_copy.wait()

    def down_sum(part, carry):
        grad_down[part] = (down_own[part, core] + down_in[part].astype(F32)).astype(BF)
        return carry

    lax.fori_loop(0, count_y, down_sum, 0)

    def gate_sum(rel, carry):
        cls = lax.rem(y + rel, 4)
        await_bytes(gate_in.at[cls], gate_recv.at[rel])
        for half in range(2):
            total = (own[rel, half, core] + gate_in[cls, half].astype(F32)).astype(BF)
            grad_gate[:, slice_of(cls + 4 * half)] = total[:units]
            grad_up[:, slice_of(cls + 4 * half)] = total[units:]
        return carry

    lax.fori_loop(0, 4, gate_sum, 0)

    await_bytes(pay_rows.at[pl.ds(0, chips - 1)], rows_send)
    await_bytes(pay_target.at[pl.ds(0, chips - 1)], target_send)
    await_bytes(rows.at[0], ring_send.at[0])
    await_bytes(rows.at[0], ring_send.at[1])
    await_bytes(rows.at[0, pl.ds(0, chips // 2)], ring_send.at[2])
    await_bytes(rows.at[0, pl.ds(0, chips // 2)], ring_send.at[3])
    await_bytes(hidden.at[pl.ds(0, count_y - 1)], hid_send)
    await_bytes(back_out.at[pl.ds(0, count_y - 1)], back_send)
    await_bytes(gate_out, gate_send)


def body(
    tokens, teacher_out, route_weight, routes, twin_map, student_gate, student_up, student_down
):
    block, topk = routes.shape
    teachers = twin_map.shape[0]
    chips = teachers // 2
    cap = 2 * block * topk // teachers
    height = 4 * cap
    feature = teacher_out.shape[2]
    width = target_width(feature)
    model = tokens.shape[1]
    units = student_gate.shape[1]
    count_y = model // feature
    slots = chips * 2 * cap
    vmem = pl.BlockSpec(memory_space=pltpu.VMEM)
    anywhere = pl.BlockSpec(memory_space=pl.ANY)
    pay_rows, pay_target = pl.pallas_call(
        pack_kernel,
        out_shape=(
            jax.ShapeDtypeStruct((chips, height, feature), BF),
            jax.ShapeDtypeStruct((chips, height, width), BF),
        ),
        in_specs=[vmem] * 6,
        out_specs=(vmem, vmem),
        compiler_params=pltpu.CompilerParams(vmem_limit_bytes=48 * 1024 * 1024),
    )(
        tokens, teacher_out, route_weight, routes,
        twin_map.reshape(teachers, 1), twin_map.reshape(1, teachers),
    )
    dma = pltpu.SemaphoreType.DMA
    grads = pl.pallas_call(
        main_kernel,
        out_shape=(
            jax.ShapeDtypeStruct((units, model), BF),
            jax.ShapeDtypeStruct((units, model), BF),
            jax.ShapeDtypeStruct((count_y, units, feature), BF),
        ),
        in_specs=[anywhere] * 5,
        out_specs=(vmem, vmem, vmem),
        scratch_shapes=[
            pltpu.VMEM((4, chips, height, feature), BF),
            pltpu.VMEM((chips, height, width), BF),
            pltpu.VMEM((2, 2, units, model), BF),
            pltpu.VMEM((count_y, 2, units, feature), BF),
            pltpu.VMEM((2, chips // XS * height, 4 * units), F32),
            pltpu.VMEM((slots, -(-4 * units // 128) * 128), F32),
            pltpu.VMEM((count_y, 2 * units, slots), BF),
            pltpu.VMEM((slots, feature), BF),
            pltpu.VMEM((count_y, 2 * units, slots), BF),
            pltpu.VMEM((count_y, 2 * units, slots), BF),
            pltpu.VMEM((count_y, 2, units, feature), F32),
            pltpu.VMEM((count_y, units, feature), BF),
            pltpu.VMEM((count_y, units, feature), BF),
            pltpu.VMEM((2, 4 * units, chips * height), BF),
            pltpu.VMEM((4, 2, 2, 2 * units, feature), F32),
            pltpu.VMEM((4, 2, 2 * units, feature), BF),
            pltpu.VMEM((4, 2, 2 * units, feature), BF),
            dma((3,)), dma((3,)), dma((3,)),
            dma((XS,)), dma, dma, dma,
            dma((XS,)), dma((XS,)), dma((XS,)), dma((XS,)), dma((4,)),
            dma, dma, dma, dma, dma, dma, dma, dma((4,)),
        ],
        compiler_params=pltpu.CompilerParams(
            collective_id=0, has_side_effects=True, vmem_limit_bytes=56 * 1024 * 1024),
    )(
        pay_rows, pay_target, student_gate[0], student_up[0],
        student_down[0].reshape(count_y, units, feature),
    )
    return (
        grads[0][None], grads[1][None], grads[2].reshape(1, count_y * units, feature))


def solution(mesh):
    placed = (
        P("expert", None),
        P("expert", None, "dp"),
        P("expert", None),
        P("expert", None),
        P(),
        P("expert", "dp", None),
        P("expert", "dp", None),
        P("expert", None, "dp"),
    )
    return jax.shard_map(
        body,
        mesh=mesh,
        in_specs=placed,
        out_specs=(P("expert", "dp", None), P("expert", "dp", None), P("expert", None, "dp")),
        check_vma=False,
    )
```

```python
import functools
import jax
import jax.numpy as jnp
from jax import lax
from jax.experimental import pallas as pl
from jax.experimental.pallas import tpu as pltpu
from jax.sharding import PartitionSpec as P

BF = jnp.bfloat16
F32 = jnp.float32
XS = 4
NT_DIMS = (((1,), (1,)), ((), ()))
TN_DIMS = (((0,), (0,)), ((), ()))


def hot(cond):
    return jnp.where(cond, 1.0, 0.0).astype(BF)


def iota(shape, dim):
    return lax.broadcasted_iota(jnp.int32, shape, dim)


def target_width(feature):
    return -(-(feature + 128) // 256) * 128


def ring_chunks(chips):
    halves = []
    for start in (0, chips // 2):
        end = start + chips // 2
        chunks = [(start, XS)]
        while sum(chunks[-1]) < end:
            first = sum(chunks[-1])
            chunks.append((first, min(2 * XS, end - first)))
        halves.append(chunks)
    return halves


def pack(tokens, teacher, weight, routes, twin, pay_rows, pay_target):
    topk, block = routes.shape
    pairs = block * topk
    teachers = twin.shape[1]
    cap = 2 * pairs // teachers
    group = 2 * cap
    width = pay_target.shape[2]
    rows = pay_rows.shape[0] * pay_rows.shape[1]

    token_of = hot(iota((pairs, block), 0) // topk == iota((pairs, block), 1))
    token_of_t = hot(iota((block, pairs), 1) // topk == iota((block, pairs), 0))
    place_col = iota((pairs, topk), 0) % topk == iota((pairs, topk), 1)
    place_row = iota((topk, pairs), 1) % topk == iota((topk, pairs), 0)
    named = routes[...].astype(F32).astype(BF)
    teach_col = jnp.sum(
        jnp.where(place_col, lax.dot_general(token_of, named, NT_DIMS, preferred_element_type=F32), 0.0),
        axis=1, keepdims=True)
    teach_row = jnp.sum(
        jnp.where(place_row, jnp.dot(named, token_of_t, preferred_element_type=F32), 0.0),
        axis=0, keepdims=True)
    weight_col = jnp.sum(
        jnp.where(
            place_col, lax.dot_general(token_of, weight[...], NT_DIMS, preferred_element_type=F32), 0.0),
        axis=1, keepdims=True)
    earlier = iota((pairs, pairs), 0) < iota((pairs, pairs), 1)
    rank_row = jnp.sum(
        jnp.where((teach_col == teach_row) & earlier, 1.0, 0.0), axis=0, keepdims=True)
    twin_row = jnp.broadcast_to(twin[...].astype(F32), (teachers, teachers))
    same = iota((teachers, teachers), 0) == iota((teachers, teachers), 1)
    twin_col = jnp.sum(jnp.where(same, twin_row, 0.0), axis=1, keepdims=True)
    before = iota((teachers, teachers), 1) < iota((teachers, teachers), 0)
    twin_of = jnp.sum(
        jnp.where((twin_col == twin_row) & before, 1.0, 0.0), axis=1, keepdims=True)
    first_slot = twin_col * float(group) + twin_of * float(cap)
    teacher_hot = iota((teachers, pairs), 0).astype(F32) == teach_row
    slot_row = rank_row + jnp.sum(jnp.where(teacher_hot, first_slot, 0.0), axis=0, keepdims=True)

    row_ids = iota((rows, pairs), 0)
    slot_of = (row_ids // (2 * group)) * group + row_ids % group
    half_of = (row_ids // group) % 2
    filled = slot_of.astype(F32) == slot_row
    put_low = hot(filled & (half_of == 0))
    put_high = hot(filled & (half_of == 1))

    spread = hot(iota((pairs, 2 * block), 0) // topk == iota((pairs, 2 * block), 1) % block)
    pick = jnp.dot(hot(filled), spread, preferred_element_type=F32)
    pick_half = iota((rows, 2 * block), 1) // block == (iota((rows, 2 * block), 0) // group) % 2
    pick = jnp.where(pick_half, pick, 0.0).astype(BF)
    sent = jnp.dot(pick, tokens[...], preferred_element_type=F32).astype(BF)
    pay_rows[...] = sent.reshape(pay_rows.shape)

    spread_weight = jnp.broadcast_to(weight_col, (pairs, 128)).astype(BF)
    tail = jnp.concatenate([teacher[:, width:], spread_weight], axis=1)
    sent = jnp.dot(put_low, teacher[:, :width], preferred_element_type=F32) + jnp.dot(
        put_high, tail, preferred_element_type=F32)
    pay_target[...] = sent.astype(BF).reshape(pay_target.shape)


def main_kernel(
    tokens, teacher, weight, routes, twin, gate, up, down,
    gate_own, gate_in, down_kept, down_in,
    own_tokens, own_teacher, own_weight, own_routes, own_twin, pay_rows, pay_target, rows, target, weights, weights_down, pre, slots_pre, hidden, err, back_out, back_in,
    down_out, down_part_both, expand, kept, gate_out, gate_both,
    in_local, w_recv, w_local, w_send, rows_recv, rows_send, target_recv, target_send,
    left_recv, right_recv, fwd_left_recv, fwd_right_recv, ring_send,
    hid_send, hid_recv, back_send, back_recv, down_send, down_recv, gate_send, gate_recv,
):
    chips = pay_rows.shape[0]
    line = chips // XS
    height = pay_rows.shape[1]
    group = height // 2
    feature = pay_rows.shape[2]
    width = pay_target.shape[2]
    tail = feature - width
    units = gate.shape[0]
    count_y = down.shape[0]
    slots = chips * group
    block = tokens.shape[0]
    me = lax.axis_index("expert")
    y = lax.axis_index("dp")
    core = lax.rem(me, 2)
    other = 1 - core
    chip = me // 2
    x = chip // line
    z = lax.rem(chip, line)
    sibling = (chip * 2 + other, y)
    right_y = lax.rem(y + 1, count_y)
    left_y = lax.rem(y + count_y - 1, count_y)
    right = (me, right_y)
    left = (me, left_y)

    def peer(step):
        dx = lax.rem(step, XS)
        turn = step // XS
        dz = jnp.where(lax.rem(turn, 2) == 1, (turn + 1) // 2, line - turn // 2)
        return lax.rem(x + XS - dx, XS) * line + lax.rem(z + 2 * line - dz, line)

    halves = ring_chunks(chips)
    chunks = halves[0] + halves[1]
    part_chips = chips // 2
    part_slots = slots // 2

    def slice_of(cls):
        return pl.ds(pl.multiple_of(cls * feature, 128), feature)

    def remote(src, dst, send_sem, recv_sem, device):
        return pltpu.make_async_remote_copy(
            src_ref=src, dst_ref=dst, send_sem=send_sem, recv_sem=recv_sem,
            device_id=device, device_id_type=pl.DeviceIdType.MESH)

    def await_bytes(ref, sem):
        pltpu.make_async_copy(ref, ref, sem).wait()

    barrier = pltpu.get_barrier_semaphore()
    pl.semaphore_signal(barrier, inc=1, device_id=sibling, device_id_type=pl.DeviceIdType.MESH)

    to_x = [lax.rem(x + XS - dx, XS) * line for dx in range(XS)]
    to_z = []
    for turn in range(line):
        dz = (turn + 1) // 2 if turn % 2 else (line - turn // 2) % line
        to_z.append(lax.rem(z + line - dz, line))

    for step in range(1, chips):
        pl.semaphore_signal(
            barrier, inc=1, device_id=((to_x[step % XS] + to_z[step // XS]) * 2 + core, y), device_id_type=pl.DeviceIdType.MESH)
    for step in range(1, count_y):
        pl.semaphore_signal(
            barrier, inc=1, device_id=(me, lax.rem(y + step, count_y)),
            device_id_type=pl.DeviceIdType.MESH)

    cls = lax.rem(y, 4)
    in_copies = [
        pltpu.make_async_copy(tokens.at[:, slice_of(cls)], own_tokens.at[pl.ds(0, block)], in_local.at[0]),
        pltpu.make_async_copy(
            tokens.at[:, slice_of(cls + 4)], own_tokens.at[pl.ds(block, block)], in_local.at[1]),
        pltpu.make_async_copy(teacher, own_teacher, in_local.at[2]),
        pltpu.make_async_copy(weight, own_weight, in_local.at[3]),
        pltpu.make_async_copy(routes, own_routes, in_local.at[4]),
        pltpu.make_async_copy(twin, own_twin, in_local.at[5]),
    ]
    for copy in in_copies:
        copy.start()
    own_copies = [
        pltpu.make_async_copy(gate, weights.at[core, 0], w_local.at[0]),
        pltpu.make_async_copy(up, weights.at[core, 1], w_local.at[1]),
        pltpu.make_async_copy(down, weights_down.at[:, core], w_local.at[2]),
    ]
    for copy in own_copies:
        copy.start()
    for copy in in_copies:
        copy.wait()
    pack(own_tokens, own_teacher, own_weight, own_routes, own_twin, pay_rows, pay_target)
    pltpu.make_async_copy(pay_rows.at[chip], rows.at[0, 0], rows_recv.at[0]).start()
    pltpu.make_async_copy(pay_target.at[chip], target.at[0], target_recv.at[0]).start()
    pl.semaphore_wait(barrier, chips - 1 + count_y - 1 + 1)

    def send_rows(number):
        def send(step, carry):
            to = peer(step)
            remote(
                pay_rows.at[to], rows.at[0, step], rows_send, rows_recv.at[number], (to * 2 + core, y)
            ).start()
            return carry

        first, count = chunks[number]
        lax.fori_loop(max(first, 1), first + count, send, 0)

    def send_target(part):
        def send(step, carry):
            to = peer(step)
            remote(
                pay_target.at[to], target.at[step], target_send, target_recv.at[part], (to * 2 + core, y)
            ).start()
            return carry

        lax.fori_loop(max(part * part_chips, 1), (part + 1) * part_chips, send, 0)

    for number in range(len(chunks)):
        send_rows(number)
    weight_copies = [
        remote(gate, weights.at[core, 0], w_send.at[0], w_recv.at[0], sibling),
        remote(up, weights.at[core, 1], w_send.at[1], w_recv.at[1], sibling),
        remote(down, weights_down.at[:, core], w_send.at[2], w_recv.at[2], sibling),
    ]
    for copy in weight_copies:
        copy.start()
    send_target(0)
    send_target(1)

    def send_own(number):
        at = pl.ds(*chunks[number])
        await_bytes(rows.at[0, at], rows_recv.at[number])
        remote(rows.at[0, at], rows.at[3, at], ring_send.at[0], left_recv.at[number], right).start()
        remote(rows.at[0, at], rows.at[1, at], ring_send.at[1], right_recv.at[number], left).start()

    def forward(number):
        start, count = chunks[number]
        at, first, last = pl.ds(start, count), pl.ds(start, count // 2), pl.ds(start + count // 2, count // 2)
        await_bytes(rows.at[3, at], left_recv.at[number])
        remote(rows.at[3, first], rows.at[2, first], ring_send.at[2], fwd_left_recv.at[number], right).start()
        await_bytes(rows.at[1, at], right_recv.at[number])
        remote(rows.at[1, last], rows.at[2, last], ring_send.at[3], fwd_right_recv.at[number], left).start()

    def project(part):
        start = part * part_chips
        for number, (first, count) in enumerate(chunks):
            if start <= first < start + part_chips:
                await_bytes(rows.at[2, pl.ds(first, count // 2)], fwd_left_recv.at[number])
                await_bytes(rows.at[2, pl.ds(first + count // 2, count // 2)], fwd_right_recv.at[number])
        pre[...] = jnp.zeros_like(pre)

        def add(rel, carry):
            cls = lax.rem(y + rel, 4)
            block = rows[rel, pl.ds(start, part_chips)].reshape(part_chips * height, feature)
            for half in range(2):
                w = weights[:, :, :, slice_of(cls + 4 * half)].reshape(4 * units, feature)
                pre[half] += lax.dot_general(block, w, NT_DIMS, preferred_element_type=F32)
            return carry

        lax.fori_loop(0, 4, add, 0)
        low = pre[0].reshape(part_chips, height, 4 * units)[:, :group]
        high = pre[1].reshape(part_chips, height, 4 * units)[:, group:]
        slots_pre[:, : 4 * units] = (low + high).reshape(part_slots, 4 * units)
        gates = slots_pre[...].T[: 4 * units].reshape(2, 2, units, part_slots)
        gate_pre = gates[:, 0].reshape(2 * units, part_slots)
        up_pre = gates[:, 1].reshape(2 * units, part_slots)
        sig = 1.0 / (1.0 + jnp.exp(-gate_pre))
        silu = gate_pre * sig
        hidden[part, y] = (silu * up_pre).astype(BF)

        def send_hidden(step, carry):
            to = lax.rem(y + step, count_y)
            remote(hidden.at[part, y], hidden.at[part, y], hid_send, hid_recv.at[part], (me, to)).start()
            return carry

        lax.fori_loop(1, count_y, send_hidden, 0)
        return silu, up_pre * sig * (1.0 + gate_pre * (1.0 - sig))

    def errors(part):
        await_bytes(target.at[pl.ds(part * part_chips, part_chips)], target_recv.at[part])
        await_bytes(hidden.at[part, pl.ds(0, count_y - 1)], hid_recv.at[part])
        all_hidden = hidden[part].reshape(count_y * 2 * units, part_slots)
        all_down = weights_down[...].reshape(count_y * 2 * units, feature)
        out = lax.dot_general(all_hidden, all_down, TN_DIMS, preferred_element_type=F32)
        arrived = target[pl.ds(part * part_chips, part_chips)].astype(F32)
        goal_low = arrived[:, :group].reshape(part_slots, width)
        goal_high = arrived[:, group:].reshape(part_slots, width)
        slot_weight = goal_high[:, tail : tail + 1]
        err[part, :, :width] = (slot_weight * (out[:, :width] - goal_low)).astype(BF)
        err[part, :, width:] = (slot_weight * (out[:, width:] - goal_high[:, :tail])).astype(BF)

        def send_back(step, carry):
            to = lax.rem(y + step, count_y)
            w = weights_down[to].reshape(2 * units, feature)
            back_out[part, to] = lax.dot_general(
                w, err[part], NT_DIMS, preferred_element_type=F32).astype(BF)

            @pl.when(step < count_y)
            def _():
                remote(
                    back_out.at[part, to], back_in.at[part, y], back_send, back_recv.at[part], (me, to)
                ).start()
            return carry

        lax.fori_loop(1, count_y + 1, send_back, 0)

    def back(part, silu, slope):
        await_bytes(back_in.at[part, pl.ds(0, count_y - 1)], back_recv.at[part])

        def add_back(step, total):
            return total + back_in[part, lax.rem(y + step, count_y)].astype(F32)

        back_hidden = lax.fori_loop(1, count_y, add_back, back_out[part, y].astype(F32))
        back_gate = (back_hidden * slope).astype(BF).reshape(2, 1, units, part_slots)
        back_up = (back_hidden * silu).astype(BF).reshape(2, 1, units, part_slots)
        backs = jnp.concatenate([back_gate, back_up], axis=1).reshape(4 * units, part_slots)
        wide = (part_slots, part_chips * height)
        for half in range(2):
            slot_id, lane = iota(wide, 0), iota(wide, 1)
            match = (lane // height == slot_id // group) & (
                lane % height == slot_id % group + group * half)
            expand[half] = jnp.dot(backs, hot(match), preferred_element_type=F32).astype(BF)

    def class_term(rel, part):
        lhs = expand[...].reshape(8 * units, part_chips * height)
        block = rows[rel, pl.ds(part * part_chips, part_chips)].reshape(part_chips * height, feature)
        return jnp.dot(lhs, block, preferred_element_type=F32)

    slots_pre[...] = jnp.zeros_like(slots_pre)
    send_own(0)
    for copy in own_copies + weight_copies:
        copy.wait()
    first_part = len(halves[0])
    for number in range(len(chunks)):
        if number + 1 < len(chunks):
            send_own(number + 1)
        forward(number)
        if number == first_part:
            saved = project(0)
        if number == first_part + 1:
            errors(0)
    if first_part + 1 >= len(chunks):
        errors(0)
    saved_last = project(1)

    back(0, *saved)

    def first_term(rel, carry):
        kept[rel] = class_term(rel, 0)
        return carry

    lax.fori_loop(0, 4, first_term, 0)
    errors(1)

    def down_part(number, carry):
        term = jnp.dot(hidden[0, number], err[0], preferred_element_type=F32) + jnp.dot(
            hidden[1, number], err[1], preferred_element_type=F32)
        down_part_both[...] = term.reshape(2, units, feature)
        down_out[number] = down_part_both[other].astype(BF)
        down_kept[number] = down_part_both[core].astype(BF)
        return carry

    lax.fori_loop(0, count_y, down_part, 0)
    down_copy = remote(down_out, down_in, down_send, down_recv, sibling)
    down_copy.start()

    back(1, *saved_last)

    def class_part(rel, carry):
        cls = lax.rem(y + rel, 4)
        gate_both[...] = (kept[rel] + class_term(rel, 1)).reshape(2, 2, 2 * units, feature)
        gate_out[cls] = gate_both[:, other].astype(BF)
        gate_own[cls] = gate_both[:, core].astype(BF)
        remote(gate_out.at[cls], gate_in.at[cls], gate_send, gate_recv.at[rel], sibling).start()
        return carry

    lax.fori_loop(0, 4, class_part, 0)
    down_copy.wait()
    for rel in range(4):
        await_bytes(gate_in.at[rel], gate_recv.at[rel])

    await_bytes(pay_rows.at[pl.ds(0, chips - 1)], rows_send)
    await_bytes(pay_target.at[pl.ds(0, chips - 1)], target_send)
    await_bytes(rows.at[0], ring_send.at[0])
    await_bytes(rows.at[0], ring_send.at[1])
    await_bytes(rows.at[0, pl.ds(0, chips // 2)], ring_send.at[2])
    await_bytes(rows.at[0, pl.ds(0, chips // 2)], ring_send.at[3])
    for part in range(2):
        await_bytes(hidden.at[part, pl.ds(0, count_y - 1)], hid_send)
        await_bytes(back_out.at[part, pl.ds(0, count_y - 1)], back_send)
    await_bytes(gate_out, gate_send)


def sum_kernel(gate_own, gate_in, down_kept, down_in, grad_gate, grad_up, grad_down):
    units = grad_gate.shape[0]
    feature = gate_own.shape[3]
    for half in range(2):
        for cls in range(4):
            at = pl.ds((cls + 4 * half) * feature, feature)
            total = (gate_own[cls, half].astype(F32) + gate_in[cls, half].astype(F32)).astype(BF)
            grad_gate[:, at] = total[:units]
            grad_up[:, at] = total[units:]
    grad_down[...] = (down_kept[...].astype(F32) + down_in[...].astype(F32)).astype(BF)


def body(
    tokens, teacher_out, route_weight, routes, twin_map, student_gate, student_up, student_down
):
    block, topk = routes.shape
    teachers = twin_map.shape[0]
    chips = teachers // 2
    cap = 2 * block * topk // teachers
    height = 4 * cap
    feature = teacher_out.shape[2]
    width = target_width(feature)
    model = tokens.shape[1]
    units = student_gate.shape[1]
    count_y = model // feature
    slots = chips * 2 * cap
    vmem = pl.BlockSpec(memory_space=pltpu.VMEM)
    anywhere = pl.BlockSpec(memory_space=pl.ANY)
    dma = pltpu.SemaphoreType.DMA
    chunks = sum(len(part) for part in ring_chunks(chips))
    parts = pl.pallas_call(
        main_kernel,
        out_shape=(
            jax.ShapeDtypeStruct((4, 2, 2 * units, feature), BF),
            jax.ShapeDtypeStruct((4, 2, 2 * units, feature), BF),
            jax.ShapeDtypeStruct((count_y, units, feature), BF),
            jax.ShapeDtypeStruct((count_y, units, feature), BF),
        ),
        in_specs=[anywhere] * 8,
        out_specs=(vmem, vmem, vmem, vmem),
        scratch_shapes=[
            pltpu.VMEM((2 * block, feature), BF),
            pltpu.VMEM((block * topk, feature), BF),
            pltpu.VMEM((topk, block), BF),
            pltpu.VMEM((topk, block), jnp.int32),
            pltpu.VMEM((1, teachers), jnp.int32),
            pltpu.VMEM((chips, height, feature), BF),
            pltpu.VMEM((chips, height, width), BF),
            pltpu.VMEM((4, chips, height, feature), BF),
            pltpu.VMEM((chips, height, width), BF),
            pltpu.VMEM((2, 2, units, model), BF),
            pltpu.VMEM((count_y, 2, units, feature), BF),
            pltpu.VMEM((2, chips // 2 * height, 4 * units), F32),
            pltpu.VMEM((slots // 2, -(-4 * units // 128) * 128), F32),
            pltpu.VMEM((2, count_y, 2 * units, slots // 2), BF),
            pltpu.VMEM((2, slots // 2, feature), BF),
            pltpu.VMEM((2, count_y, 2 * units, slots // 2), BF),
            pltpu.VMEM((2, count_y, 2 * units, slots // 2), BF),
            pltpu.VMEM((count_y, units, feature), BF),
            pltpu.VMEM((2, units, feature), F32),
            pltpu.VMEM((2, 4 * units, chips // 2 * height), BF),
            pltpu.VMEM((4, 8 * units, feature), F32),
            pltpu.VMEM((4, 2, 2 * units, feature), BF),
            pltpu.VMEM((2, 2, 2 * units, feature), F32),
            dma((6,)), dma((3,)), dma((3,)), dma((3,)),
            dma((chunks,)), dma, dma((2,)), dma,
            dma((chunks,)), dma((chunks,)), dma((chunks,)), dma((chunks,)), dma((4,)),
            dma, dma((2,)), dma, dma((2,)), dma, dma, dma, dma((4,)),
        ],
        compiler_params=pltpu.CompilerParams(
            collective_id=0, has_side_effects=True, vmem_limit_bytes=60 * 1024 * 1024),
    )(
        tokens, teacher_out.reshape(block * topk, feature), route_weight.T, routes.T,
        twin_map.reshape(1, teachers), student_gate[0], student_up[0],
        student_down[0].reshape(count_y, units, feature),
    )
    grads = pl.pallas_call(
        sum_kernel,
        out_shape=(
            jax.ShapeDtypeStruct((units, model), BF),
            jax.ShapeDtypeStruct((units, model), BF),
            jax.ShapeDtypeStruct((count_y, units, feature), BF),
        ),
        in_specs=[vmem] * 4,
        out_specs=(vmem, vmem, vmem),
        compiler_params=pltpu.CompilerParams(vmem_limit_bytes=60 * 1024 * 1024),
    )(*parts)
    return (
        grads[0][None], grads[1][None], grads[2].reshape(1, count_y * units, feature))


def solution(mesh):
    placed = (
        P("expert", None),
        P("expert", None, "dp"),
        P("expert", None),
        P("expert", None),
        P(),
        P("expert", "dp", None),
        P("expert", "dp", None),
        P("expert", None, "dp"),
    )
    return jax.shard_map(
        body,
        mesh=mesh,
        in_specs=placed,
        out_specs=(P("expert", "dp", None), P("expert", "dp", None), P("expert", None, "dp")),
        check_vma=False,
    )
```

```python
import functools
import jax
import jax.numpy as jnp
from jax import lax
from jax.experimental import pallas as pl
from jax.experimental.pallas import tpu as pltpu
from jax.sharding import PartitionSpec as P

BF = jnp.bfloat16
F32 = jnp.float32
XS = 4
NT_DIMS = (((1,), (1,)), ((), ()))
TN_DIMS = (((0,), (0,)), ((), ()))


def hot(cond):
    return jnp.where(cond, 1.0, 0.0).astype(BF)


def iota(shape, dim):
    return lax.broadcasted_iota(jnp.int32, shape, dim)


def target_width(feature):
    return -(-(feature + 128) // 256) * 128


def ring_chunks(chips):
    halves = []
    for start in (0, chips // 2):
        end = start + chips // 2
        chunks = [(start, XS)]
        while sum(chunks[-1]) < end:
            first = sum(chunks[-1])
            chunks.append((first, min(2 * XS, end - first)))
        halves.append(chunks)
    return halves


def pack(tokens, teacher, weight, routes, twin, pay_rows, pay_more, pay_target):
    topk, block = routes.shape
    pairs = block * topk
    teachers = twin.shape[1]
    cap = 2 * pairs // teachers
    group = 2 * cap
    width = pay_target.shape[2]
    rows = pay_rows.shape[0] * pay_rows.shape[1]

    token_of = hot(iota((pairs, block), 0) // topk == iota((pairs, block), 1))
    token_of_t = hot(iota((block, pairs), 1) // topk == iota((block, pairs), 0))
    place_col = iota((pairs, topk), 0) % topk == iota((pairs, topk), 1)
    place_row = iota((topk, pairs), 1) % topk == iota((topk, pairs), 0)
    named = routes[...].astype(F32).astype(BF)
    teach_col = jnp.sum(
        jnp.where(place_col, lax.dot_general(token_of, named, NT_DIMS, preferred_element_type=F32), 0.0),
        axis=1, keepdims=True)
    teach_row = jnp.sum(
        jnp.where(place_row, jnp.dot(named, token_of_t, preferred_element_type=F32), 0.0),
        axis=0, keepdims=True)
    weight_col = jnp.sum(
        jnp.where(
            place_col, lax.dot_general(token_of, weight[...], NT_DIMS, preferred_element_type=F32), 0.0),
        axis=1, keepdims=True)
    earlier = iota((pairs, pairs), 0) < iota((pairs, pairs), 1)
    rank_row = jnp.sum(
        jnp.where((teach_col == teach_row) & earlier, 1.0, 0.0), axis=0, keepdims=True)
    twin_row = jnp.broadcast_to(twin[...].astype(F32), (teachers, teachers))
    same = iota((teachers, teachers), 0) == iota((teachers, teachers), 1)
    twin_col = jnp.sum(jnp.where(same, twin_row, 0.0), axis=1, keepdims=True)
    before = iota((teachers, teachers), 1) < iota((teachers, teachers), 0)
    twin_of = jnp.sum(
        jnp.where((twin_col == twin_row) & before, 1.0, 0.0), axis=1, keepdims=True)
    first_slot = twin_col * float(group) + twin_of * float(cap)
    teacher_hot = iota((teachers, pairs), 0).astype(F32) == teach_row
    slot_row = rank_row + jnp.sum(jnp.where(teacher_hot, first_slot, 0.0), axis=0, keepdims=True)

    row_ids = iota((rows, pairs), 0)
    slot_of = (row_ids // (2 * group)) * group + row_ids % group
    half_of = (row_ids // group) % 2
    filled = slot_of.astype(F32) == slot_row
    put_low = hot(filled & (half_of == 0))
    put_high = hot(filled & (half_of == 1))

    spread = hot(iota((pairs, 2 * block), 0) // topk == iota((pairs, 2 * block), 1) % block)
    pick = jnp.dot(hot(filled), spread, preferred_element_type=F32)
    pick_half = iota((rows, 2 * block), 1) // block == (iota((rows, 2 * block), 0) // group) % 2
    pick = jnp.where(pick_half, pick, 0.0).astype(BF)
    for number, pay in enumerate((pay_rows, pay_more)):
        both = tokens[pl.ds(number * 2 * block, 2 * block), :]
        sent = jnp.dot(pick, both, preferred_element_type=F32).astype(BF)
        pay[...] = sent.reshape(pay.shape)

    spread_weight = jnp.broadcast_to(weight_col, (pairs, 128)).astype(BF)
    tail = jnp.concatenate([teacher[:, width:], spread_weight], axis=1)
    sent = jnp.dot(put_low, teacher[:, :width], preferred_element_type=F32) + jnp.dot(
        put_high, tail, preferred_element_type=F32)
    pay_target[...] = sent.astype(BF).reshape(pay_target.shape)


def main_kernel(
    tokens, teacher, weight, routes, twin, gate, up, down,
    gate_own, gate_in, down_kept, down_in,
    own_tokens, own_teacher, own_weight, own_routes, own_twin, pay_rows, pay_more, pay_target, rows, target, weights, weights_down, pre, slots_pre, hidden, err, back_out, back_in,
    down_out, down_mine, down_part_both, expand, kept, gate_out, gate_mine, gate_both,
    in_local, w_recv, w_local, w_send, rows_recv, rows_send, target_recv, target_send,
    left_recv, right_recv, fwd_left_recv, fwd_right_recv, ring_send,
    more_send, more_recv, out_sem,
    hid_send, hid_recv, back_send, back_recv, down_send, down_recv, gate_send, gate_recv,
):
    chips = pay_rows.shape[0]
    line = chips // XS
    height = pay_rows.shape[1]
    group = height // 2
    feature = pay_rows.shape[2]
    width = pay_target.shape[2]
    tail = feature - width
    units = gate.shape[0]
    count_y = down.shape[0]
    slots = chips * group
    block = tokens.shape[0]
    me = lax.axis_index("expert")
    y = lax.axis_index("dp")
    core = lax.rem(me, 2)
    other = 1 - core
    chip = me // 2
    x = chip // line
    z = lax.rem(chip, line)
    sibling = (chip * 2 + other, y)
    right_y = lax.rem(y + 1, count_y)
    left_y = lax.rem(y + count_y - 1, count_y)
    right = (me, right_y)
    left = (me, left_y)

    def peer(step):
        if isinstance(step, int):
            return to_x[step % XS] + to_z[step // XS]
        dx = lax.rem(step, XS)
        turn = step // XS
        dz = jnp.where(lax.rem(turn, 2) == 1, (turn + 1) // 2, line - turn // 2)
        return lax.rem(x + XS - dx, XS) * line + lax.rem(z + 2 * line - dz, line)

    halves = ring_chunks(chips)
    chunks = halves[0] + halves[1]
    direct = sum(halves[0][min(1, len(halves[0]) - 1)])
    part_chips = chips // 2
    part_slots = slots // 2

    def slice_of(cls):
        return pl.ds(pl.multiple_of(cls * feature, 128), feature)

    def remote(src, dst, send_sem, recv_sem, device):
        return pltpu.make_async_remote_copy(
            src_ref=src, dst_ref=dst, send_sem=send_sem, recv_sem=recv_sem,
            device_id=device, device_id_type=pl.DeviceIdType.MESH)

    def await_bytes(ref, sem):
        pltpu.make_async_copy(ref, ref, sem).wait()

    barrier = pltpu.get_barrier_semaphore()
    pl.semaphore_signal(barrier, inc=1, device_id=sibling, device_id_type=pl.DeviceIdType.MESH)

    to_x = [lax.rem(x + XS - dx, XS) * line for dx in range(XS)]
    to_z = []
    for turn in range(line):
        dz = (turn + 1) // 2 if turn % 2 else (line - turn // 2) % line
        to_z.append(lax.rem(z + line - dz, line))

    for step in range(1, chips):
        pl.semaphore_signal(
            barrier, inc=1, device_id=((to_x[step % XS] + to_z[step // XS]) * 2 + core, y), device_id_type=pl.DeviceIdType.MESH)
    for step in range(1, count_y):
        pl.semaphore_signal(
            barrier, inc=1, device_id=(me, lax.rem(y + step, count_y)),
            device_id_type=pl.DeviceIdType.MESH)

    cls = lax.rem(y, 4)
    far = lax.rem(y + 2, 4)
    in_copies = [
        pltpu.make_async_copy(
            tokens.at[:, slice_of(first)], own_tokens.at[pl.ds(number * block, block)],
            in_local.at[4 + number])
        for number, first in enumerate((cls, cls + 4, far, far + 4))
    ] + [
        pltpu.make_async_copy(teacher, own_teacher, in_local.at[0]),
        pltpu.make_async_copy(weight, own_weight, in_local.at[1]),
        pltpu.make_async_copy(routes, own_routes, in_local.at[2]),
        pltpu.make_async_copy(twin, own_twin, in_local.at[3]),
    ]
    for copy in in_copies:
        copy.start()
    own_copies = [
        pltpu.make_async_copy(gate, weights.at[core, 0], w_local.at[0]),
        pltpu.make_async_copy(up, weights.at[core, 1], w_local.at[1]),
        pltpu.make_async_copy(down, weights_down.at[:, core], w_local.at[2]),
    ]
    for copy in own_copies:
        copy.start()
    for copy in in_copies:
        copy.wait()
    pack(own_tokens, own_teacher, own_weight, own_routes, own_twin, pay_rows, pay_more, pay_target)
    pltpu.make_async_copy(pay_rows.at[chip], rows.at[0, 0], rows_recv.at[0]).start()
    pltpu.make_async_copy(pay_more.at[chip], rows.at[2, 0], more_recv).start()
    pltpu.make_async_copy(pay_target.at[chip], target.at[0], target_recv.at[0]).start()
    pl.semaphore_wait(barrier, chips - 1 + count_y - 1 + 1)

    def send_rows(number):
        first, count = chunks[number]
        for step in range(max(first, 1), first + count):
            to = peer(step)
            remote(
                pay_rows.at[to], rows.at[0, step], rows_send, rows_recv.at[number], (to * 2 + core, y)
            ).start()

    def send_target(part):
        def send(step, carry):
            to = peer(step)
            remote(
                pay_target.at[to], target.at[step], target_send, target_recv.at[part], (to * 2 + core, y)
            ).start()
            return carry

        lax.fori_loop(max(part * part_chips, 1), (part + 1) * part_chips, send, 0)

    def send_more():
        for step in range(1, direct):
            to = peer(step)
            remote(
                pay_more.at[to], rows.at[2, step], more_send, more_recv, (to * 2 + core, y)
            ).start()

    weight_copies = [
        remote(gate, weights.at[core, 0], w_send.at[0], w_recv.at[0], sibling),
        remote(up, weights.at[core, 1], w_send.at[1], w_recv.at[1], sibling),
        remote(down, weights_down.at[:, core], w_send.at[2], w_recv.at[2], sibling),
    ]

    def send_weights():
        for copy in weight_copies:
            copy.start()

    def await_weights():
        for copy in own_copies + weight_copies:
            copy.wait()

    def send_own(number):
        at = pl.ds(*chunks[number])
        await_bytes(rows.at[0, at], rows_recv.at[number])
        remote(rows.at[0, at], rows.at[3, at], ring_send.at[0], left_recv.at[number], right).start()
        remote(rows.at[0, at], rows.at[1, at], ring_send.at[1], right_recv.at[number], left).start()

    def forward(number):
        start, count = chunks[number]
        if start < direct:
            return
        at, first, last = pl.ds(start, count), pl.ds(start, count // 2), pl.ds(start + count // 2, count // 2)
        await_bytes(rows.at[3, at], left_recv.at[number])
        remote(rows.at[3, first], rows.at[2, first], ring_send.at[2], fwd_left_recv.at[number], right).start()
        await_bytes(rows.at[1, at], right_recv.at[number])
        remote(rows.at[1, last], rows.at[2, last], ring_send.at[3], fwd_right_recv.at[number], left).start()

    def project(part):
        start = part * part_chips
        for number, (first, count) in enumerate(chunks):
            if start <= first < min(start + part_chips, direct):
                await_bytes(rows.at[3, pl.ds(first, count)], left_recv.at[number])
                await_bytes(rows.at[1, pl.ds(first, count)], right_recv.at[number])
        pre[...] = jnp.zeros_like(pre)

        def add(turn, carry):
            rel = turn + turn // 2
            add_class(rel)
            return carry

        def add_class(rel):
            cls = lax.rem(y + rel, 4)
            block = rows[rel, pl.ds(start, part_chips)].reshape(part_chips * height, feature)
            for half in range(2):
                w = weights[:, :, :, slice_of(cls + 4 * half)].reshape(4 * units, feature)
                pre[half] += lax.dot_general(block, w, NT_DIMS, preferred_element_type=F32)

        lax.fori_loop(0, 3, add, 0)
        if part == 0:
            await_bytes(rows.at[2, pl.ds(0, direct)], more_recv)
        for number, (first, count) in enumerate(chunks):
            if max(start, direct) <= first < start + part_chips:
                await_bytes(rows.at[2, pl.ds(first, count // 2)], fwd_left_recv.at[number])
                await_bytes(rows.at[2, pl.ds(first + count // 2, count // 2)], fwd_right_recv.at[number])
        add_class(2)
        low = pre[0].reshape(part_chips, height, 4 * units)[:, :group]
        high = pre[1].reshape(part_chips, height, 4 * units)[:, group:]
        slots_pre[:, : 4 * units] = (low + high).reshape(part_slots, 4 * units)
        gates = slots_pre[...].T[: 4 * units].reshape(2, 2, units, part_slots)
        gate_pre = gates[:, 0].reshape(2 * units, part_slots)
        up_pre = gates[:, 1].reshape(2 * units, part_slots)
        sig = 1.0 / (1.0 + jnp.exp(-gate_pre))
        silu = gate_pre * sig
        hidden[part, y] = (silu * up_pre).astype(BF)

        def send_hidden(step, carry):
            to = lax.rem(y + step, count_y)
            remote(hidden.at[part, y], hidden.at[part, y], hid_send, hid_recv.at[part], (me, to)).start()
            return carry

        lax.fori_loop(1, count_y, send_hidden, 0)
        return silu, up_pre * sig * (1.0 + gate_pre * (1.0 - sig))

    def errors(part):
        await_bytes(target.at[pl.ds(part * part_chips, part_chips)], target_recv.at[part])
        await_bytes(hidden.at[part, pl.ds(0, count_y - 1)], hid_recv.at[part])
        all_hidden = hidden[part].reshape(count_y * 2 * units, part_slots)
        all_down = weights_down[...].reshape(count_y * 2 * units, feature)
        out = lax.dot_general(all_hidden, all_down, TN_DIMS, preferred_element_type=F32)
        arrived = target[pl.ds(part * part_chips, part_chips)].astype(F32)
        goal_low = arrived[:, :group].reshape(part_slots, width)
        goal_high = arrived[:, group:].reshape(part_slots, width)
        slot_weight = goal_high[:, tail : tail + 1]
        err[part, :, :width] = (slot_weight * (out[:, :width] - goal_low)).astype(BF)
        err[part, :, width:] = (slot_weight * (out[:, width:] - goal_high[:, :tail])).astype(BF)

        def send_back(step, carry):
            to = lax.rem(y + step, count_y)
            w = weights_down[to].reshape(2 * units, feature)
            back_out[part, to] = lax.dot_general(
                w, err[part], NT_DIMS, preferred_element_type=F32).astype(BF)

            @pl.when(step < count_y)
            def _():
                remote(
                    back_out.at[part, to], back_in.at[part, y], back_send, back_recv.at[part], (me, to)
                ).start()
            return carry

        lax.fori_loop(1, count_y + 1, send_back, 0)

    def back(part, silu, slope):
        await_bytes(back_in.at[part, pl.ds(0, count_y - 1)], back_recv.at[part])

        def add_back(step, total):
            return total + back_in[part, lax.rem(y + step, count_y)].astype(F32)

        back_hidden = lax.fori_loop(1, count_y, add_back, back_out[part, y].astype(F32))
        back_gate = (back_hidden * slope).astype(BF).reshape(2, 1, units, part_slots)
        back_up = (back_hidden * silu).astype(BF).reshape(2, 1, units, part_slots)
        backs = jnp.concatenate([back_gate, back_up], axis=1).reshape(4 * units, part_slots)
        wide = (part_slots, part_chips * height)
        for half in range(2):
            slot_id, lane = iota(wide, 0), iota(wide, 1)
            match = (lane // height == slot_id // group) & (
                lane % height == slot_id % group + group * half)
            expand[half] = jnp.dot(backs, hot(match), preferred_element_type=F32).astype(BF)

    def class_term(rel, part):
        lhs = expand[...].reshape(8 * units, part_chips * height)
        block = rows[rel, pl.ds(part * part_chips, part_chips)].reshape(part_chips * height, feature)
        return jnp.dot(lhs, block, preferred_element_type=F32)

    slots_pre[...] = jnp.zeros_like(slots_pre)
    last = len(chunks) - 1
    for number in range(last):
        send_rows(number)
    send_more()
    send_rows(last)
    send_own(0)
    send_weights()
    for number in range(1, min(3, last + 1)):
        send_own(number)
    send_target(0)
    await_weights()
    for number in range(min(3, last + 1)):
        if number == 2:
            send_own(3)
        forward(number)
    send_target(1)
    for number in range(3, last):
        send_own(number + 1)
        forward(number)
        if number == 3:
            saved = project(0)
    if last < 4:
        saved = project(0)
    if last > 2:
        forward(last)
    errors(0)
    saved_last = project(1)

    back(0, *saved)

    def first_term(rel, carry):
        kept[rel] = class_term(rel, 0)
        return carry

    lax.fori_loop(0, 4, first_term, 0)
    errors(1)

    def down_part(number, carry):
        term = jnp.dot(hidden[0, number], err[0], preferred_element_type=F32) + jnp.dot(
            hidden[1, number], err[1], preferred_element_type=F32)
        down_part_both[...] = term.reshape(2, units, feature)
        down_out[number] = down_part_both[other].astype(BF)
        down_mine[number] = down_part_both[core].astype(BF)
        return carry

    lax.fori_loop(0, count_y, down_part, 0)
    down_copy = remote(down_out, down_in, down_send, down_recv, sibling)
    down_copy.start()
    kept_copy = pltpu.make_async_copy(down_mine, down_kept, out_sem.at[4])
    kept_copy.start()

    back(1, *saved_last)

    def class_part(rel, carry):
        cls = lax.rem(y + rel, 4)
        gate_both[...] = (kept[rel] + class_term(rel, 1)).reshape(2, 2, 2 * units, feature)
        gate_out[cls] = gate_both[:, other].astype(BF)
        gate_mine[rel] = gate_both[:, core].astype(BF)
        pltpu.make_async_copy(gate_mine.at[rel], gate_own.at[cls], out_sem.at[rel]).start()
        remote(gate_out.at[cls], gate_in.at[cls], gate_send, gate_recv.at[rel], sibling).start()
        return carry

    lax.fori_loop(0, 4, class_part, 0)
    down_copy.wait()
    kept_copy.wait()
    for rel in range(4):
        cls = lax.rem(y + rel, 4)
        pltpu.make_async_copy(gate_mine.at[rel], gate_own.at[cls], out_sem.at[rel]).wait()
        await_bytes(gate_in.at[cls], gate_recv.at[rel])

    await_bytes(pay_rows.at[pl.ds(0, chips - 1)], rows_send)
    await_bytes(pay_target.at[pl.ds(0, chips - 1)], target_send)
    await_bytes(rows.at[0], ring_send.at[0])
    await_bytes(rows.at[0], ring_send.at[1])
    await_bytes(rows.at[0, pl.ds(0, (chips - direct) // 2)], ring_send.at[2])
    await_bytes(rows.at[0, pl.ds(0, (chips - direct) // 2)], ring_send.at[3])
    await_bytes(pay_more.at[pl.ds(0, direct - 1)], more_send)
    for part in range(2):
        await_bytes(hidden.at[part, pl.ds(0, count_y - 1)], hid_send)
        await_bytes(back_out.at[part, pl.ds(0, count_y - 1)], back_send)
    await_bytes(gate_out, gate_send)


def sum_kernel(gate_own, gate_in, down_kept, down_in, grad_gate, grad_up, grad_down):
    units = grad_gate.shape[0]
    feature = gate_own.shape[3]
    for half in range(2):
        for cls in range(4):
            at = pl.ds((cls + 4 * half) * feature, feature)
            total = (gate_own[cls, half].astype(F32) + gate_in[cls, half].astype(F32)).astype(BF)
            grad_gate[:, at] = total[:units]
            grad_up[:, at] = total[units:]
    grad_down[...] = (down_kept[...].astype(F32) + down_in[...].astype(F32)).astype(BF)


def body(
    tokens, teacher_out, route_weight, routes, twin_map, student_gate, student_up, student_down
):
    block, topk = routes.shape
    teachers = twin_map.shape[0]
    chips = teachers // 2
    cap = 2 * block * topk // teachers
    height = 4 * cap
    feature = teacher_out.shape[2]
    width = target_width(feature)
    model = tokens.shape[1]
    units = student_gate.shape[1]
    count_y = model // feature
    slots = chips * 2 * cap
    vmem = pl.BlockSpec(memory_space=pltpu.VMEM)
    anywhere = pl.BlockSpec(memory_space=pl.ANY)
    dma = pltpu.SemaphoreType.DMA
    chunks = sum(len(part) for part in ring_chunks(chips))
    parts = pl.pallas_call(
        main_kernel,
        out_shape=(
            jax.ShapeDtypeStruct((4, 2, 2 * units, feature), BF),
            jax.ShapeDtypeStruct((4, 2, 2 * units, feature), BF),
            jax.ShapeDtypeStruct((count_y, units, feature), BF),
            jax.ShapeDtypeStruct((count_y, units, feature), BF),
        ),
        in_specs=[anywhere] * 8,
        out_specs=(anywhere,) * 4,
        scratch_shapes=[
            pltpu.VMEM((4 * block, feature), BF),
            pltpu.VMEM((block * topk, feature), BF),
            pltpu.VMEM((topk, block), BF),
            pltpu.VMEM((topk, block), jnp.int32),
            pltpu.VMEM((1, teachers), jnp.int32),
            pltpu.VMEM((chips, height, feature), BF),
            pltpu.VMEM((chips, height, feature), BF),
            pltpu.VMEM((chips, height, width), BF),
            pltpu.VMEM((4, chips, height, feature), BF),
            pltpu.VMEM((chips, height, width), BF),
            pltpu.VMEM((2, 2, units, model), BF),
            pltpu.VMEM((count_y, 2, units, feature), BF),
            pltpu.VMEM((2, chips // 2 * height, 4 * units), F32),
            pltpu.VMEM((slots // 2, -(-4 * units // 128) * 128), F32),
            pltpu.VMEM((2, count_y, 2 * units, slots // 2), BF),
            pltpu.VMEM((2, slots // 2, feature), BF),
            pltpu.VMEM((2, count_y, 2 * units, slots // 2), BF),
            pltpu.VMEM((2, count_y, 2 * units, slots // 2), BF),
            pltpu.VMEM((count_y, units, feature), BF),
            pltpu.VMEM((count_y, units, feature), BF),
            pltpu.VMEM((2, units, feature), F32),
            pltpu.VMEM((2, 4 * units, chips // 2 * height), BF),
            pltpu.VMEM((4, 8 * units, feature), F32),
            pltpu.VMEM((4, 2, 2 * units, feature), BF),
            pltpu.VMEM((4, 2, 2 * units, feature), BF),
            pltpu.VMEM((2, 2, 2 * units, feature), F32),
            dma((8,)), dma((3,)), dma((3,)), dma((3,)),
            dma((chunks,)), dma, dma((2,)), dma,
            dma((chunks,)), dma((chunks,)), dma((chunks,)), dma((chunks,)), dma((4,)),
            dma, dma, dma((5,)),
            dma, dma((2,)), dma, dma((2,)), dma, dma, dma, dma((4,)),
        ],
        compiler_params=pltpu.CompilerParams(
            collective_id=0, has_side_effects=True, vmem_limit_bytes=60 * 1024 * 1024),
    )(
        tokens, teacher_out.reshape(block * topk, feature), route_weight.T, routes.T,
        twin_map.reshape(1, teachers), student_gate[0], student_up[0],
        student_down[0].reshape(count_y, units, feature),
    )
    grads = pl.pallas_call(
        sum_kernel,
        out_shape=(
            jax.ShapeDtypeStruct((units, model), BF),
            jax.ShapeDtypeStruct((units, model), BF),
            jax.ShapeDtypeStruct((count_y, units, feature), BF),
        ),
        in_specs=[vmem] * 4,
        out_specs=(vmem, vmem, vmem),
        compiler_params=pltpu.CompilerParams(vmem_limit_bytes=60 * 1024 * 1024),
    )(*parts)
    return (
        grads[0][None], grads[1][None], grads[2].reshape(1, count_y * units, feature))


def solution(mesh):
    placed = (
        P("expert", None),
        P("expert", None, "dp"),
        P("expert", None),
        P("expert", None),
        P(),
        P("expert", "dp", None),
        P("expert", "dp", None),
        P("expert", None, "dp"),
    )
    return jax.shard_map(
        body,
        mesh=mesh,
        in_specs=placed,
        out_specs=(P("expert", "dp", None), P("expert", "dp", None), P("expert", None, "dp")),
        check_vma=False,
    )
```

```python
import functools
import jax
import jax.numpy as jnp
from jax import lax
from jax.experimental import pallas as pl
from jax.experimental.pallas import tpu as pltpu
from jax.sharding import PartitionSpec as P

BF = jnp.bfloat16
F32 = jnp.float32
XS = 4
NT_DIMS = (((1,), (1,)), ((), ()))
TN_DIMS = (((0,), (0,)), ((), ()))


def hot(cond):
    return jnp.where(cond, 1.0, 0.0).astype(BF)


def iota(shape, dim):
    return lax.broadcasted_iota(jnp.int32, shape, dim)


def target_width(feature):
    return -(-(feature + 128) // 256) * 128


def ring_chunks(chips):
    halves = []
    for start in (0, chips // 2):
        end = start + chips // 2
        chunks = [(start, XS)]
        while sum(chunks[-1]) < end:
            first = sum(chunks[-1])
            chunks.append((first, min(2 * XS, end - first)))
        halves.append(chunks)
    return halves


def pack(tokens, teacher, weight, routes, twin, pay_rows, pay_more, pay_target):
    topk, block = routes.shape
    pairs = block * topk
    teachers = twin.shape[1]
    cap = 2 * pairs // teachers
    group = 2 * cap
    width = pay_target.shape[2]
    rows = pay_rows.shape[0] * pay_rows.shape[1]

    token_of = hot(iota((pairs, block), 0) // topk == iota((pairs, block), 1))
    token_of_t = hot(iota((block, pairs), 1) // topk == iota((block, pairs), 0))
    place_col = iota((pairs, topk), 0) % topk == iota((pairs, topk), 1)
    place_row = iota((topk, pairs), 1) % topk == iota((topk, pairs), 0)
    named = routes[...].astype(F32).astype(BF)
    teach_col = jnp.sum(
        jnp.where(place_col, lax.dot_general(token_of, named, NT_DIMS, preferred_element_type=F32), 0.0),
        axis=1, keepdims=True)
    teach_row = jnp.sum(
        jnp.where(place_row, jnp.dot(named, token_of_t, preferred_element_type=F32), 0.0),
        axis=0, keepdims=True)
    weight_col = jnp.sum(
        jnp.where(
            place_col, lax.dot_general(token_of, weight[...], NT_DIMS, preferred_element_type=F32), 0.0),
        axis=1, keepdims=True)
    earlier = iota((pairs, pairs), 0) < iota((pairs, pairs), 1)
    rank_row = jnp.sum(
        jnp.where((teach_col == teach_row) & earlier, 1.0, 0.0), axis=0, keepdims=True)
    twin_row = jnp.broadcast_to(twin[...].astype(F32), (teachers, teachers))
    same = iota((teachers, teachers), 0) == iota((teachers, teachers), 1)
    twin_col = jnp.sum(jnp.where(same, twin_row, 0.0), axis=1, keepdims=True)
    before = iota((teachers, teachers), 1) < iota((teachers, teachers), 0)
    twin_of = jnp.sum(
        jnp.where((twin_col == twin_row) & before, 1.0, 0.0), axis=1, keepdims=True)
    first_slot = twin_col * float(group) + twin_of * float(cap)
    teacher_hot = iota((teachers, pairs), 0).astype(F32) == teach_row
    slot_row = rank_row + jnp.sum(jnp.where(teacher_hot, first_slot, 0.0), axis=0, keepdims=True)

    row_ids = iota((rows, pairs), 0)
    slot_of = (row_ids // (2 * group)) * group + row_ids % group
    half_of = (row_ids // group) % 2
    filled = slot_of.astype(F32) == slot_row
    put_low = hot(filled & (half_of == 0))
    put_high = hot(filled & (half_of == 1))

    spread = hot(iota((pairs, 2 * block), 0) // topk == iota((pairs, 2 * block), 1) % block)
    pick = jnp.dot(hot(filled), spread, preferred_element_type=F32)
    pick_half = iota((rows, 2 * block), 1) // block == (iota((rows, 2 * block), 0) // group) % 2
    pick = jnp.where(pick_half, pick, 0.0).astype(BF)
    for number, pay in enumerate((pay_rows, pay_more)):
        both = tokens[pl.ds(number * 2 * block, 2 * block), :]
        sent = jnp.dot(pick, both, preferred_element_type=F32).astype(BF)
        pay[...] = sent.reshape(pay.shape)

    spread_weight = jnp.broadcast_to(weight_col, (pairs, 128)).astype(BF)
    tail = jnp.concatenate([teacher[:, width:], spread_weight], axis=1)
    sent = jnp.dot(put_low, teacher[:, :width], preferred_element_type=F32) + jnp.dot(
        put_high, tail, preferred_element_type=F32)
    pay_target[...] = sent.astype(BF).reshape(pay_target.shape)


def main_kernel(
    tokens, teacher, weight, routes, twin, gate, up, down,
    gate_own, gate_in, down_kept, down_in,
    own_tokens, own_teacher, own_weight, own_routes, own_twin, pay_rows, pay_more, pay_target, rows, target, weights, weights_down, pre, slots_pre, hidden, err, back_out, back_in,
    down_out, down_mine, down_part_both, expand, kept, gate_out, gate_mine, gate_both,
    in_local, w_recv, w_local, w_send, rows_recv, rows_send, target_recv, target_send,
    left_recv, right_recv, fwd_left_recv, fwd_right_recv, ring_send,
    more_send, more_recv, out_sem,
    hid_send, hid_recv, back_send, back_recv, down_send, down_recv, gate_send, gate_recv,
):
    chips = pay_rows.shape[0]
    line = chips // XS
    height = pay_rows.shape[1]
    group = height // 2
    feature = pay_rows.shape[2]
    width = pay_target.shape[2]
    tail = feature - width
    units = gate.shape[0]
    count_y = down.shape[0]
    slots = chips * group
    block = tokens.shape[0]
    me = lax.axis_index("expert")
    y = lax.axis_index("dp")
    core = lax.rem(me, 2)
    other = 1 - core
    chip = me // 2
    x = chip // line
    z = lax.rem(chip, line)
    sibling = (chip * 2 + other, y)
    right_y = lax.rem(y + 1, count_y)
    left_y = lax.rem(y + count_y - 1, count_y)
    right = (me, right_y)
    left = (me, left_y)

    def peer(step):
        if isinstance(step, int):
            return to_x[step % XS] + to_z[step // XS]
        dx = lax.rem(step, XS)
        turn = step // XS
        dz = jnp.where(lax.rem(turn, 2) == 1, (turn + 1) // 2, line - turn // 2)
        return lax.rem(x + XS - dx, XS) * line + lax.rem(z + 2 * line - dz, line)

    halves = ring_chunks(chips)
    chunks = halves[0] + halves[1]
    direct = sum(halves[0][min(1, len(halves[0]) - 1)])
    part_chips = chips // 2
    part_slots = slots // 2

    def slice_of(cls):
        return pl.ds(pl.multiple_of(cls * feature, 128), feature)

    def remote(src, dst, send_sem, recv_sem, device):
        return pltpu.make_async_remote_copy(
            src_ref=src, dst_ref=dst, send_sem=send_sem, recv_sem=recv_sem,
            device_id=device, device_id_type=pl.DeviceIdType.MESH)

    def await_bytes(ref, sem):
        pltpu.make_async_copy(ref, ref, sem).wait()

    barrier = pltpu.get_barrier_semaphore()
    pl.semaphore_signal(barrier, inc=1, device_id=sibling, device_id_type=pl.DeviceIdType.MESH)

    to_x = [lax.rem(x + XS - dx, XS) * line for dx in range(XS)]
    to_z = []
    for turn in range(line):
        dz = (turn + 1) // 2 if turn % 2 else (line - turn // 2) % line
        to_z.append(lax.rem(z + line - dz, line))

    for step in range(1, chips):
        pl.semaphore_signal(
            barrier, inc=1, device_id=((to_x[step % XS] + to_z[step // XS]) * 2 + core, y), device_id_type=pl.DeviceIdType.MESH)
    for step in range(1, count_y):
        pl.semaphore_signal(
            barrier, inc=1, device_id=(me, lax.rem(y + step, count_y)),
            device_id_type=pl.DeviceIdType.MESH)

    cls = lax.rem(y, 4)
    far = lax.rem(y + 2, 4)
    in_copies = [
        pltpu.make_async_copy(
            tokens.at[:, slice_of(first)], own_tokens.at[pl.ds(number * block, block)],
            in_local.at[4 + number])
        for number, first in enumerate((cls, cls + 4, far, far + 4))
    ] + [
        pltpu.make_async_copy(teacher, own_teacher, in_local.at[0]),
        pltpu.make_async_copy(weight, own_weight, in_local.at[1]),
        pltpu.make_async_copy(routes, own_routes, in_local.at[2]),
        pltpu.make_async_copy(twin, own_twin, in_local.at[3]),
    ]
    for copy in in_copies:
        copy.start()
    own_copies = [
        pltpu.make_async_copy(gate, weights.at[core, 0], w_local.at[0]),
        pltpu.make_async_copy(up, weights.at[core, 1], w_local.at[1]),
        pltpu.make_async_copy(down, weights_down.at[:, core], w_local.at[2]),
    ]
    for copy in own_copies:
        copy.start()
    for copy in in_copies:
        copy.wait()
    pack(own_tokens, own_teacher, own_weight, own_routes, own_twin, pay_rows, pay_more, pay_target)
    pltpu.make_async_copy(pay_rows.at[chip], rows.at[0, 0], rows_recv.at[0]).start()
    pltpu.make_async_copy(pay_more.at[chip], rows.at[2, 0], more_recv).start()
    pltpu.make_async_copy(pay_target.at[chip], target.at[0], target_recv.at[0]).start()
    pl.semaphore_wait(barrier, chips - 1 + count_y - 1 + 1)

    def send_rows(number):
        first, count = chunks[number]
        for step in range(max(first, 1), first + count):
            to = peer(step)
            remote(
                pay_rows.at[to], rows.at[0, step], rows_send, rows_recv.at[number], (to * 2 + core, y)
            ).start()

    def send_target(part):
        def send(step, carry):
            to = peer(step)
            remote(
                pay_target.at[to], target.at[step], target_send, target_recv.at[part], (to * 2 + core, y)
            ).start()
            return carry

        lax.fori_loop(max(part * part_chips, 1), (part + 1) * part_chips, send, 0)

    def send_more():
        for step in range(1, direct):
            to = peer(step)
            remote(
                pay_more.at[to], rows.at[2, step], more_send, more_recv, (to * 2 + core, y)
            ).start()

    weight_copies = [
        remote(gate, weights.at[core, 0], w_send.at[0], w_recv.at[0], sibling),
        remote(up, weights.at[core, 1], w_send.at[1], w_recv.at[1], sibling),
        remote(down, weights_down.at[:, core], w_send.at[2], w_recv.at[2], sibling),
    ]

    def send_weights():
        for copy in weight_copies:
            copy.start()

    def await_weights():
        for copy in own_copies + weight_copies:
            copy.wait()

    def send_own(number):
        at = pl.ds(*chunks[number])
        await_bytes(rows.at[0, at], rows_recv.at[number])
        remote(rows.at[0, at], rows.at[3, at], ring_send.at[0], left_recv.at[number], right).start()
        remote(rows.at[0, at], rows.at[1, at], ring_send.at[1], right_recv.at[number], left).start()

    def forward(number):
        start, count = chunks[number]
        if start < direct:
            return
        at, first, last = pl.ds(start, count), pl.ds(start, count // 2), pl.ds(start + count // 2, count // 2)
        await_bytes(rows.at[3, at], left_recv.at[number])
        remote(rows.at[3, first], rows.at[2, first], ring_send.at[2], fwd_left_recv.at[number], right).start()
        await_bytes(rows.at[1, at], right_recv.at[number])
        remote(rows.at[1, last], rows.at[2, last], ring_send.at[3], fwd_right_recv.at[number], left).start()

    def project(part):
        start = part * part_chips
        for number, (first, count) in enumerate(chunks):
            if start <= first < min(start + part_chips, direct):
                await_bytes(rows.at[3, pl.ds(first, count)], left_recv.at[number])
                await_bytes(rows.at[1, pl.ds(first, count)], right_recv.at[number])
        pre[...] = jnp.zeros_like(pre)

        def add(turn, carry):
            rel = turn + turn // 2
            add_class(rel)
            return carry

        def add_class(rel):
            cls = lax.rem(y + rel, 4)
            block = rows[rel, pl.ds(start, part_chips)].reshape(part_chips * height, feature)
            for half in range(2):
                w = weights[:, :, :, slice_of(cls + 4 * half)].reshape(4 * units, feature)
                pre[half] += lax.dot_general(block, w, NT_DIMS, preferred_element_type=F32)

        lax.fori_loop(0, 3, add, 0)
        if part == 0:
            await_bytes(rows.at[2, pl.ds(0, direct)], more_recv)
        for number, (first, count) in enumerate(chunks):
            if max(start, direct) <= first < start + part_chips:
                await_bytes(rows.at[2, pl.ds(first, count // 2)], fwd_left_recv.at[number])
                await_bytes(rows.at[2, pl.ds(first + count // 2, count // 2)], fwd_right_recv.at[number])
        add_class(2)
        low = pre[0].reshape(part_chips, height, 4 * units)[:, :group]
        high = pre[1].reshape(part_chips, height, 4 * units)[:, group:]
        slots_pre[:, : 4 * units] = (low + high).reshape(part_slots, 4 * units)
        gates = slots_pre[...].T[: 4 * units].reshape(2, 2, units, part_slots)
        gate_pre = gates[:, 0].reshape(2 * units, part_slots)
        up_pre = gates[:, 1].reshape(2 * units, part_slots)
        sig = 1.0 / (1.0 + jnp.exp(-gate_pre))
        silu = gate_pre * sig
        hidden[part, y] = (silu * up_pre).astype(BF)

        def send_hidden(step, carry):
            to = lax.rem(y + step, count_y)
            remote(hidden.at[part, y], hidden.at[part, y], hid_send, hid_recv.at[part], (me, to)).start()
            return carry

        lax.fori_loop(1, count_y, send_hidden, 0)
        return silu, up_pre * sig * (1.0 + gate_pre * (1.0 - sig))

    def errors(part):
        await_bytes(target.at[pl.ds(part * part_chips, part_chips)], target_recv.at[part])
        await_bytes(hidden.at[part, pl.ds(0, count_y - 1)], hid_recv.at[part])
        all_hidden = hidden[part].reshape(count_y * 2 * units, part_slots)
        all_down = weights_down[...].reshape(count_y * 2 * units, feature)
        out = lax.dot_general(all_hidden, all_down, TN_DIMS, preferred_element_type=F32)
        arrived = target[pl.ds(part * part_chips, part_chips)].astype(F32)
        goal_low = arrived[:, :group].reshape(part_slots, width)
        goal_high = arrived[:, group:].reshape(part_slots, width)
        slot_weight = goal_high[:, tail : tail + 1]
        err[part, :, :width] = (slot_weight * (out[:, :width] - goal_low)).astype(BF)
        err[part, :, width:] = (slot_weight * (out[:, width:] - goal_high[:, :tail])).astype(BF)

        def send_back(step, carry):
            to = lax.rem(y + step, count_y)
            w = weights_down[to].reshape(2 * units, feature)
            back_out[part, to] = lax.dot_general(
                w, err[part], NT_DIMS, preferred_element_type=F32).astype(BF)

            @pl.when(step < count_y)
            def _():
                remote(
                    back_out.at[part, to], back_in.at[part, y], back_send, back_recv.at[part], (me, to)
                ).start()
            return carry

        lax.fori_loop(1, count_y + 1, send_back, 0)

    def back(part, silu, slope):
        await_bytes(back_in.at[part, pl.ds(0, count_y - 1)], back_recv.at[part])

        def add_back(step, total):
            return total + back_in[part, lax.rem(y + step, count_y)].astype(F32)

        back_hidden = lax.fori_loop(1, count_y, add_back, back_out[part, y].astype(F32))
        back_gate = (back_hidden * slope).astype(BF).reshape(2, 1, units, part_slots)
        back_up = (back_hidden * silu).astype(BF).reshape(2, 1, units, part_slots)
        backs = jnp.concatenate([back_gate, back_up], axis=1).reshape(4 * units, part_slots)
        wide = (part_slots, part_chips * height)
        for half in range(2):
            slot_id, lane = iota(wide, 0), iota(wide, 1)
            match = (lane // height == slot_id // group) & (
                lane % height == slot_id % group + group * half)
            expand[half] = jnp.dot(backs, hot(match), preferred_element_type=F32).astype(BF)

    def class_term(rel, part):
        lhs = expand[...].reshape(8 * units, part_chips * height)
        block = rows[rel, pl.ds(part * part_chips, part_chips)].reshape(part_chips * height, feature)
        return jnp.dot(lhs, block, preferred_element_type=F32)

    slots_pre[...] = jnp.zeros_like(slots_pre)
    last = len(chunks) - 1
    for number in range(last):
        send_rows(number)
    send_more()
    send_rows(last)
    send_own(0)
    send_weights()
    for number in range(1, min(3, last + 1)):
        send_own(number)
    send_target(0)
    await_weights()
    for number in range(min(3, last + 1)):
        if number == 2:
            send_own(3)
        forward(number)
    for number in range(3, last):
        send_own(number + 1)
        forward(number)
        if number == 3:
            send_target(1)
            saved = project(0)
    if last < 4:
        send_target(1)
        saved = project(0)
    if last > 2:
        forward(last)
    errors(0)
    saved_last = project(1)

    back(0, *saved)

    def first_term(rel, carry):
        kept[rel] = class_term(rel, 0)
        return carry

    lax.fori_loop(0, 4, first_term, 0)
    errors(1)

    def down_part(number, carry):
        term = jnp.dot(hidden[0, number], err[0], preferred_element_type=F32) + jnp.dot(
            hidden[1, number], err[1], preferred_element_type=F32)
        down_part_both[...] = term.reshape(2, units, feature)
        down_out[number] = down_part_both[other].astype(BF)
        down_mine[number] = down_part_both[core].astype(BF)
        return carry

    lax.fori_loop(0, count_y, down_part, 0)
    down_copy = remote(down_out, down_in, down_send, down_recv, sibling)
    down_copy.start()
    kept_copy = pltpu.make_async_copy(down_mine, down_kept, out_sem.at[4])
    kept_copy.start()

    back(1, *saved_last)

    def class_part(rel, carry):
        cls = lax.rem(y + rel, 4)
        gate_both[...] = (kept[rel] + class_term(rel, 1)).reshape(2, 2, 2 * units, feature)
        gate_out[cls] = gate_both[:, other].astype(BF)
        gate_mine[rel] = gate_both[:, core].astype(BF)
        pltpu.make_async_copy(gate_mine.at[rel], gate_own.at[cls], out_sem.at[rel]).start()
        remote(gate_out.at[cls], gate_in.at[cls], gate_send, gate_recv.at[rel], sibling).start()
        return carry

    lax.fori_loop(0, 4, class_part, 0)
    down_copy.wait()
    kept_copy.wait()
    for rel in range(4):
        cls = lax.rem(y + rel, 4)
        pltpu.make_async_copy(gate_mine.at[rel], gate_own.at[cls], out_sem.at[rel]).wait()
        await_bytes(gate_in.at[cls], gate_recv.at[rel])

    await_bytes(pay_rows.at[pl.ds(0, chips - 1)], rows_send)
    await_bytes(pay_target.at[pl.ds(0, chips - 1)], target_send)
    await_bytes(rows.at[0], ring_send.at[0])
    await_bytes(rows.at[0], ring_send.at[1])
    await_bytes(rows.at[0, pl.ds(0, (chips - direct) // 2)], ring_send.at[2])
    await_bytes(rows.at[0, pl.ds(0, (chips - direct) // 2)], ring_send.at[3])
    await_bytes(pay_more.at[pl.ds(0, direct - 1)], more_send)
    for part in range(2):
        await_bytes(hidden.at[part, pl.ds(0, count_y - 1)], hid_send)
        await_bytes(back_out.at[part, pl.ds(0, count_y - 1)], back_send)
    await_bytes(gate_out, gate_send)


def sum_kernel(gate_own, gate_in, down_kept, down_in, grad_gate, grad_up, grad_down):
    units = grad_gate.shape[0]
    feature = gate_own.shape[3]
    for half in range(2):
        for cls in range(4):
            at = pl.ds((cls + 4 * half) * feature, feature)
            total = (gate_own[cls, half].astype(F32) + gate_in[cls, half].astype(F32)).astype(BF)
            grad_gate[:, at] = total[:units]
            grad_up[:, at] = total[units:]
    grad_down[...] = (down_kept[...].astype(F32) + down_in[...].astype(F32)).astype(BF)


def body(
    tokens, teacher_out, route_weight, routes, twin_map, student_gate, student_up, student_down
):
    block, topk = routes.shape
    teachers = twin_map.shape[0]
    chips = teachers // 2
    cap = 2 * block * topk // teachers
    height = 4 * cap
    feature = teacher_out.shape[2]
    width = target_width(feature)
    model = tokens.shape[1]
    units = student_gate.shape[1]
    count_y = model // feature
    slots = chips * 2 * cap
    vmem = pl.BlockSpec(memory_space=pltpu.VMEM)
    anywhere = pl.BlockSpec(memory_space=pl.ANY)
    dma = pltpu.SemaphoreType.DMA
    chunks = sum(len(part) for part in ring_chunks(chips))
    parts = pl.pallas_call(
        main_kernel,
        out_shape=(
            jax.ShapeDtypeStruct((4, 2, 2 * units, feature), BF),
            jax.ShapeDtypeStruct((4, 2, 2 * units, feature), BF),
            jax.ShapeDtypeStruct((count_y, units, feature), BF),
            jax.ShapeDtypeStruct((count_y, units, feature), BF),
        ),
        in_specs=[anywhere] * 8,
        out_specs=(anywhere,) * 4,
        scratch_shapes=[
            pltpu.VMEM((4 * block, feature), BF),
            pltpu.VMEM((block * topk, feature), BF),
            pltpu.VMEM((topk, block), BF),
            pltpu.VMEM((topk, block), jnp.int32),
            pltpu.VMEM((1, teachers), jnp.int32),
            pltpu.VMEM((chips, height, feature), BF),
            pltpu.VMEM((chips, height, feature), BF),
            pltpu.VMEM((chips, height, width), BF),
            pltpu.VMEM((4, chips, height, feature), BF),
            pltpu.VMEM((chips, height, width), BF),
            pltpu.VMEM((2, 2, units, model), BF),
            pltpu.VMEM((count_y, 2, units, feature), BF),
            pltpu.VMEM((2, chips // 2 * height, 4 * units), F32),
            pltpu.VMEM((slots // 2, -(-4 * units // 128) * 128), F32),
            pltpu.VMEM((2, count_y, 2 * units, slots // 2), BF),
            pltpu.VMEM((2, slots // 2, feature), BF),
            pltpu.VMEM((2, count_y, 2 * units, slots // 2), BF),
            pltpu.VMEM((2, count_y, 2 * units, slots // 2), BF),
            pltpu.VMEM((count_y, units, feature), BF),
            pltpu.VMEM((count_y, units, feature), BF),
            pltpu.VMEM((2, units, feature), F32),
            pltpu.VMEM((2, 4 * units, chips // 2 * height), BF),
            pltpu.VMEM((4, 8 * units, feature), F32),
            pltpu.VMEM((4, 2, 2 * units, feature), BF),
            pltpu.VMEM((4, 2, 2 * units, feature), BF),
            pltpu.VMEM((2, 2, 2 * units, feature), F32),
            dma((8,)), dma((3,)), dma((3,)), dma((3,)),
            dma((chunks,)), dma, dma((2,)), dma,
            dma((chunks,)), dma((chunks,)), dma((chunks,)), dma((chunks,)), dma((4,)),
            dma, dma, dma((5,)),
            dma, dma((2,)), dma, dma((2,)), dma, dma, dma, dma((4,)),
        ],
        compiler_params=pltpu.CompilerParams(
            collective_id=0, has_side_effects=True, vmem_limit_bytes=60 * 1024 * 1024),
    )(
        tokens, teacher_out.reshape(block * topk, feature), route_weight.T, routes.T,
        twin_map.reshape(1, teachers), student_gate[0], student_up[0],
        student_down[0].reshape(count_y, units, feature),
    )
    grads = pl.pallas_call(
        sum_kernel,
        out_shape=(
            jax.ShapeDtypeStruct((units, model), BF),
            jax.ShapeDtypeStruct((units, model), BF),
            jax.ShapeDtypeStruct((count_y, units, feature), BF),
        ),
        in_specs=[vmem] * 4,
        out_specs=(vmem, vmem, vmem),
        compiler_params=pltpu.CompilerParams(vmem_limit_bytes=60 * 1024 * 1024),
    )(*parts)
    return (
        grads[0][None], grads[1][None], grads[2].reshape(1, count_y * units, feature))


def solution(mesh):
    placed = (
        P("expert", None),
        P("expert", None, "dp"),
        P("expert", None),
        P("expert", None),
        P(),
        P("expert", "dp", None),
        P("expert", "dp", None),
        P("expert", None, "dp"),
    )
    return jax.shard_map(
        body,
        mesh=mesh,
        in_specs=placed,
        out_specs=(P("expert", "dp", None), P("expert", "dp", None), P("expert", None, "dp")),
        check_vma=False,
    )
```
